256 devices in a mesh: dp: 8 (over y_hi, x), cent: 32 (over z, y_lo, core).
Axes of the slice: x: 4, y: 4 (y_hi: 2, y_lo: 2; y = y_hi * 2 + y_lo), z: 8, core: 2. Of those that a mesh axis runs over, the one named last changes fastest.
Arguments:
- minibatch: bfloat16 [16384, 768], P(('dp', 'cent')), may hold values from -80 to 80
- centroids: float32 [32768, 768], P('cent'), may hold values from -40 to 40
Outputs:
- refined: float32 [32768, 768], P('cent')
- log_partition: float32 [16384], P('dp')
The draws below stay inside these ranges and needn't reach their ends.
All inputs are finite; a program needn't handle non-finite values.
Results may differ from the reference program's by a relative error of at most 0.0013.
Values may be sent and summed in bfloat16 or wider, within the bound.
A program may use at most 64 MiB of HBM per device.

```python
import jax
import jax.numpy as jnp
from jax import lax

D = 768
K = 32768
N_DEV = 2048
ITERS = 2
N = 16384
N_DP = 8


def shared_groups(key):
    members = 64
    count = K // members
    mean_key, member_key = jax.random.split(key)
    means = jax.random.normal(mean_key, (count, D), jnp.float32)
    member = jax.random.permutation(member_key, K) // members
    return (means, member, count)


def draw_minibatch(key, part):
    means, member, count = shared_groups(key)
    key = jax.random.fold_in(key, 11)
    first, second = jax.random.split(key, 2)
    owner = jax.random.randint(first, (N,), 0, count)
    noise = jax.random.normal(second, (N, D), jnp.float32)
    rows = jnp.take(means, owner, axis=0) + noise
    return jnp.clip(rows, -80.0, 80.0).astype(jnp.bfloat16)


def draw_centroids(key, part):
    means, member, count = shared_groups(key)
    key = jax.random.fold_in(key, 23)
    first = jax.random.fold_in(key, 0)
    noise = jax.random.normal(first, (K, D), jnp.float32)
    values = jnp.take(means, member, axis=0) + noise
    return jnp.clip(values, -40.0, 40.0)


def setup_inputs(seed: int = 0) -> dict:
    arg_keys = jax.random.split(jax.random.key(seed), 3)
    minibatch = draw_minibatch(jax.random.fold_in(arg_keys[2], 71), 0)
    centroids = draw_centroids(jax.random.fold_in(arg_keys[2], 71), 0)
    return dict(minibatch=minibatch, centroids=centroids)


INV_TEMP = 20.0
PRIOR = 0.5
EPS = 1e-06

def rms_unit(values):
    wide = values.astype(jnp.float32)
    return wide * lax.rsqrt(lax.optimization_barrier(jnp.mean(wide * wide, axis=-1, keepdims=True)) + EPS)

def reference(minibatch, centroids):
    unit_rows = rms_unit(minibatch).astype(jnp.bfloat16)
    blocks = unit_rows.reshape(N_DP, N_DEV, D)
    centers = rms_unit(centroids)
    factor = INV_TEMP / D
    log_total = jnp.zeros((N_DP, N_DEV), jnp.float32)
    for step in range(ITERS):
        center_bf = centers.astype(jnp.bfloat16)

        def visit(carry, block):
            numer, mass = carry
            scores = lax.dot_general(block, center_bf, (((1,), (1,)), ((), ())), preferred_element_type=jnp.float32) * factor
            expo = jnp.exp(scores - INV_TEMP)
            total = lax.optimization_barrier(jnp.sum(expo, axis=1))
            probs = (expo / total[:, None]).astype(jnp.bfloat16)
            numer = numer + lax.dot_general(probs, block, (((0,), (0,)), ((), ())), preferred_element_type=jnp.float32)
            mass = mass + lax.optimization_barrier(jnp.sum(probs, axis=0, dtype=jnp.float32))
            return ((numer, mass), jnp.log(total))
        start = (jnp.zeros((K, D), jnp.float32), jnp.zeros((K,), jnp.float32))
        (numer, mass), log_total = lax.scan(visit, start, blocks)
        centers = (numer + PRIOR * centers) / (mass + PRIOR)[:, None]
    return (centers, log_total.reshape(N))
```

```python
import functools

import jax
import jax.numpy as jnp
from jax import lax
from jax.experimental import pallas as pl
from jax.experimental.pallas import tpu as pltpu
from jax.sharding import PartitionSpec as P

MESH = pl.DeviceIdType.MESH
ITERS = 2
INV_TEMP = 20.0
PRIOR = 0.5
EPS = 1e-06
LOG2E = 1.4426950408889634
NX, NY, NZ, NC = 4, 4, 8, 2
BLOCK = 64
HALF = BLOCK // 2
CHUNK = 256
NCHUNK = 16
KC = 128
KD = NX * KC
D = 768
BF = jnp.bfloat16
F32 = jnp.float32


def encode(v):
    s = v * v
    return (v * jnp.abs(v) * s).astype(BF)


def decode(code):
    y = code.astype(F32)
    r = lax.rsqrt(jnp.maximum(jnp.abs(y), 1e-37))
    return y * (r * r * lax.rsqrt(r))


def body(
    mb, cents, out, tot_out,
    rows, cen_in, cb, c_own, expo, probs, macc, tp, ar_a, ar_b, ar_c, ar_u, tot, inv,
    num_own, sb, ms, rb, mr, coded,
    gs, gr, cs, cr, as_, ar, bs, br, zs, zr, ds_, dr, rs_s, rs_r, ms_s, ms_r, ag_s, ag_r, fs, fr, loc, os_,
):
    dp, ce = lax.axis_index("dp"), lax.axis_index("cent")
    yh, x = dp // 4, lax.rem(dp, 4)
    z, yl, c = ce // 4, lax.rem(ce, 4) // 2, lax.rem(ce, 2)
    y = yh * 2 + yl

    def dev(dy=0, dx=0, dz=0, dc=0):
        yy, xx = lax.rem(y + dy + NY, NY), lax.rem(x + dx + NX, NX)
        zz, cc = lax.rem(z + dz + NZ, NZ), lax.rem(c + dc, NC)
        return ((yy // 2) * 4 + xx, zz * 4 + lax.rem(yy, 2) * 2 + cc)

    def copy(src, dst, ss, rs, to):
        return pltpu.make_async_remote_copy(
            src_ref=src, dst_ref=dst, send_sem=ss, recv_sem=rs, device_id=to, device_id_type=MESH
        )

    peers = [dict(dc=1)]
    peers += [dict(dy=d) for d in (1, 2, 3)]
    peers += [dict(dx=d) for d in (1, 2, 3)]
    peers += [dict(dz=d) for d in range(1, NZ)]
    barrier = pltpu.get_barrier_semaphore()
    for p in peers:
        pl.semaphore_signal(barrier, inc=1, device_id=dev(**p), device_id_type=MESH)
    load = pltpu.make_async_copy(cents.at[pl.ds(yh * KD, KD)], cen_in, loc)
    load.start()

    def unit(v):
        return v * lax.rsqrt(jnp.mean(v * v, axis=-1, keepdims=True) + EPS)

    rows[yh, z, yl, c] = unit(mb[...].astype(F32)).astype(BF)
    pl.semaphore_wait(barrier, len(peers))

    def blk(dy, dz, half=None):
        yy = lax.rem(y + dy + NY, NY)
        r = rows.at[yy // 2, lax.rem(z + dz + NZ, NZ), lax.rem(yy, 2), c]
        return r if half is None else r.at[pl.ds(half * HALF, HALF)]

    def rsem(dy, dz, half=None):
        return gr.at[dy % NY, dz % NZ, half or 0]

    def lane(first_z):
        sends = []

        def send(dy, dz, ey, ez, half=None):
            cp = copy(
                blk(dy, dz, half), blk(dy, dz, half), gs.at[len(sends)],
                rsem(dy - ey, dz - ez, half), dev(dy=ey, dz=ez),
            )
            cp.start()
            sends.append(cp)

        def landed(dy, dz, half=None):
            b = blk(dy, dz, half)
            copy(b, b, gs.at[0], rsem(dy, dz, half), dev(dc=1)).wait_recv()

        def twin(dy, dz):
            i, j = dy % NY, dz % NZ
            copy(blk(dy, dz), blk(dy, dz), cs.at[i, j], cr.at[i, j], dev(dc=1)).start()

        def along_z(dy, dz):
            if dz == 0:
                send(dy, 0, 0, 1)
                send(dy, 0, 0, -1)
            elif abs(dz) < 3:
                send(dy, dz, 0, 1 if dz < 0 else -1)
            elif abs(dz) == 3:
                send(dy, dz, 0, 1 if dz < 0 else -1, 0 if dz < 0 else 1)

        def along_y(dy, dz):
            if dy == 0:
                send(0, dz, 1, 0)
                send(0, dz, -1, 0)
            elif abs(dy) == 1:
                send(dy, dz, 1 if dy < 0 else -1, 0, 0 if dy < 0 else 1)

        zorder = [0, -1, 1, -2, 2, -3, 3, 4]
        yorder = [0, -1, 1, 2]

        def arrive(dy, dz, halves):
            if halves:
                landed(dy, dz, 0)
                landed(dy, dz, 1)
            else:
                landed(dy, dz)

        if first_z:
            along_z(0, 0)
            along_y(0, 0)
            twin(0, 0)
            for s in range(1, 5):
                for dz in (4,) if s == 4 else (-s, s):
                    arrive(0, dz, dz == 4)
                    along_z(0, dz)
                    along_y(0, dz)
                    twin(0, dz)
                for dz in (0,) if s == 1 else (1 - s, s - 1):
                    for dy in (-1, 1):
                        arrive(dy, dz, False)
                        along_y(dy, dz)
                        twin(dy, dz)
            for dy in (-1, 1):
                arrive(dy, 4, False)
                along_y(dy, 4)
                twin(dy, 4)
            for dz in zorder:
                arrive(2, dz, True)
                twin(2, dz)
        else:
            along_y(0, 0)
            along_z(0, 0)
            twin(0, 0)
            for dy in (-1, 1, 2):
                arrive(dy, 0, dy == 2)
                along_y(dy, 0)
                along_z(dy, 0)
                twin(dy, 0)
            for s in range(1, 5):
                for dy in yorder:
                    for dz in (4,) if s == 4 else (-s, s):
                        arrive(dy, dz, dz == 4)
                        along_z(dy, dz)
                        twin(dy, dz)
        for cp in sends:
            cp.wait_send()

    @pl.when(c == 0)
    def _():
        lane(True)

    @pl.when(c == 1)
    def _():
        lane(False)

    load.wait()
    for j in range(NX):
        cb[0, j] = unit(cen_in[pl.ds(j * KC, KC)]).astype(BF)
    c_own[...] = unit(cen_in[pl.ds(x * KC, KC)])

    for i in range(NY):
        for j in range(NZ):
            yy, zz = lax.rem(y + i, NY), lax.rem(z + j, NZ)
            mine = rows.at[yy // 2, zz, lax.rem(yy, 2), c]
            his = rows.at[yy // 2, zz, lax.rem(yy, 2), 1 - c]
            copy(mine, mine, cs.at[i, j], cr.at[i, j], dev(dc=1)).wait_send()
            copy(his, his, cs.at[i, j], cr.at[i, j], dev(dc=1)).wait_recv()

    scale = INV_TEMP / D * LOG2E
    shift = INV_TEMP * LOG2E

    def chunk_rows(i):
        return rows[i // NZ, lax.rem(i, NZ)].reshape(CHUNK, D)

    for it in range(ITERS):
        def score(i, carry):
            s = lax.dot_general(
                cb[it].reshape(KD, D), chunk_rows(i), (((1,), (1,)), ((), ())), preferred_element_type=F32
            )
            e = jnp.exp2(s * scale - shift)
            expo[i] = e
            tp[i // NZ, pl.ds(lax.rem(i, NZ), 1)] = jnp.sum(e, axis=0, keepdims=True)
            return carry

        lax.fori_loop(0, NCHUNK, score, 0)

        a = copy(tp.at[1 - c], ar_a.at[it], as_.at[it], ar.at[it], dev(dc=1))
        a.start()
        a.wait_recv()
        ar_b[it, y] = tp[c] + ar_a[it]
        cps = []
        for d in (2, 1, 3):
            cps.append(copy(ar_b.at[it, y], ar_b.at[it, y], bs.at[it, d], br.at[it, d], dev(dy=d)))
            cps[-1].start()
        for d in (1, 3, 2):
            yy = lax.rem(y + NY - d, NY)
            copy(ar_b.at[it, yy], ar_b.at[it, yy], bs.at[it, d], br.at[it, d], dev(dy=d)).wait_recv()
        ar_c[it, z] = (ar_b[it, 0] + ar_b[it, 1]) + (ar_b[it, 2] + ar_b[it, 3])
        for d in (4, 3, 5, 2, 6, 1, 7):
            cps.append(copy(ar_c.at[it, z], ar_c.at[it, z], zs.at[it, d], zr.at[it, d], dev(dz=d)))
            cps[-1].start()
        for d in (1, 7, 2, 6, 3, 5, 4):
            zz = lax.rem(z + NZ - d, NZ)
            copy(ar_c.at[it, zz], ar_c.at[it, zz], zs.at[it, d], zr.at[it, d], dev(dz=d)).wait_recv()
        t = ar_c[it, 0]
        for k in range(1, NZ):
            t = t + ar_c[it, k]
        tot[it, c] = t
        back = copy(tot.at[it, c], tot.at[it, c], ds_.at[it], dr.at[it], dev(dc=1))
        back.start()
        copy(tot.at[it, 1 - c], tot.at[it, 1 - c], ds_.at[it], dr.at[it], dev(dc=1)).wait_recv()
        inv[...] = 1.0 / tot[it]
        cps += [a, back]

        def normalise(i, carry):
            p = (expo[i] * inv[i // NZ, pl.ds(lax.rem(i, NZ), 1)]).astype(BF)
            probs[i] = p
            w = p.astype(F32)
            w = w[:, :128] + w[:, 128:]
            macc[...] = jnp.where(i == 0, w, macc[...] + w)
            return carry

        lax.fori_loop(0, NCHUNK, normalise, 0)

        for d in (2, 1, 3, 0):
            j = lax.rem(x + d, NX)
            first = pl.multiple_of(j * KC, KC)

            def add(i, carry):
                n = lax.dot_general(
                    probs[i, pl.ds(first, KC)], chunk_rows(i), (((1,), (0,)), ((), ())),
                    preferred_element_type=F32,
                )
                num_own[...] = jnp.where(i == 0, n, num_own[...] + n)
                return carry

            lax.fori_loop(0, NCHUNK, add, 0)
            mass = jnp.sum(macc[pl.ds(first, KC)], axis=1, keepdims=True)
            if d:
                sb[it, d - 1] = encode(num_own[...])
                ms[it, d - 1] = jnp.broadcast_to(mass, (KC, 128)).T[:8]
                for src, dst, s1, s2 in ((sb, rb, rs_s, rs_r), (ms, mr, ms_s, ms_r)):
                    cps.append(copy(src.at[it, d - 1], dst.at[it, d - 1], s1.at[it, d], s2.at[it, d], dev(dx=d)))
                    cps[-1].start()

        num = num_own[...]
        rowm = jnp.zeros((8, 128), F32)
        for d in (1, 3, 2):
            copy(sb.at[it, d - 1], rb.at[it, d - 1], rs_s.at[it, d], rs_r.at[it, d], dev(dx=d)).wait_recv()
            copy(ms.at[it, d - 1], mr.at[it, d - 1], ms_s.at[it, d], ms_r.at[it, d], dev(dx=d)).wait_recv()
            num = num + decode(rb[it, d - 1])
            rowm = rowm + mr[it, d - 1]
        mass = mass + jnp.broadcast_to(rowm[:1], (KC, 128)).T[:, :1]
        new = (num + PRIOR * c_own[...]) * (1.0 / (mass + PRIOR))

        if it < ITERS - 1:
            c_own[...] = new
            cb[it + 1, x] = new.astype(BF)
            for d in (2, 1, 3):
                cps.append(copy(cb.at[it + 1, x], cb.at[it + 1, x], ag_s.at[it, d], ag_r.at[it, d], dev(dx=d)))
                cps[-1].start()
            for d in (1, 3, 2):
                xx = lax.rem(x + NX - d, NX)
                copy(cb.at[it + 1, xx], cb.at[it + 1, xx], ag_s.at[it, d], ag_r.at[it, d], dev(dx=d)).wait_recv()
        else:
            coded[yh, x] = encode(new)

            def slot(other, d):
                return coded.at[1 - yh if other else yh, lax.rem(x + d + NX, NX)]

            def go(other, d, k, **to):
                cps.append(copy(slot(other, d), slot(other, d), fs.at[k], fr.at[k], dev(**to)))
                cps[-1].start()

            def come(other, d, k):
                copy(slot(other, d), slot(other, d), fs.at[k], fr.at[k], dev(dc=1)).wait_recv()

            stores = []

            def store(other, d):
                s = slot(other, d)
                o = out.at[1 - yh if other else yh, lax.rem(x + d + NX, NX)]
                stores.append(pltpu.make_async_copy(s, o, os_.at[len(stores)]))
                stores[-1].start()

            go(False, 0, 0, dy=2)
            go(False, 0, 1, dx=1)
            go(False, 0, 2, dx=-1)
            go(False, 0, 3, dx=2)
            tot_out[...] = tot[it, yh]
            store(False, 0)
            come(False, 1, 2)
            go(False, 1, 4, dy=2)
            store(False, 1)
            come(False, -1, 1)
            store(False, -1)
            come(True, 0, 0)
            go(True, 0, 5, dx=1)
            store(True, 0)
            come(True, 1, 4)
            go(True, 1, 6, dx=-1)
            store(True, 1)
            come(False, 2, 3)
            store(False, 2)
            come(True, -1, 5)
            store(True, -1)
            come(True, 2, 6)
            store(True, 2)
            for st in stores:
                st.wait()
        for cp in cps:
            cp.wait_send()


def on_device(minibatch, centroids):
    dma = pltpu.SemaphoreType.DMA
    coded, total = pl.pallas_call(
        body,
        out_shape=(
            jax.ShapeDtypeStruct((2, NX, KC, D), BF),
            jax.ShapeDtypeStruct((NZ, CHUNK), F32),
        ),
        in_specs=[pl.BlockSpec(memory_space=pltpu.VMEM), pl.BlockSpec(memory_space=pl.ANY)],
        out_specs=(pl.BlockSpec(memory_space=pl.ANY), pl.BlockSpec(memory_space=pltpu.VMEM)),
        scratch_shapes=[
            pltpu.VMEM((2, NZ, 2, NC, BLOCK, D), BF),
            pltpu.VMEM((KD, D), F32),
            pltpu.VMEM((ITERS, NX, KC, D), BF),
            pltpu.VMEM((KC, D), F32),
            pltpu.VMEM((NCHUNK, KD, CHUNK), F32),
            pltpu.VMEM((NCHUNK, KD, CHUNK), BF),
            pltpu.VMEM((KD, 128), F32),
            pltpu.VMEM((2, NZ, CHUNK), F32),
            pltpu.VMEM((ITERS, NZ, CHUNK), F32),
            pltpu.VMEM((ITERS, NY, NZ, CHUNK), F32),
            pltpu.VMEM((ITERS, NZ, NZ, CHUNK), F32),
            pltpu.VMEM((NZ, CHUNK), F32),
            pltpu.VMEM((ITERS, 2, NZ, CHUNK), F32),
            pltpu.VMEM((2, NZ, CHUNK), F32),
            pltpu.VMEM((KC, D), F32),
            pltpu.VMEM((ITERS, 3, KC, D), BF),
            pltpu.VMEM((ITERS, 3, 8, 128), F32),
            pltpu.VMEM((ITERS, 3, KC, D), BF),
            pltpu.VMEM((ITERS, 3, 8, 128), F32),
            pltpu.VMEM((2, NX, KC, D), BF),
            dma((40,)), dma((NY, NZ, 2)),
            dma((NY, NZ)), dma((NY, NZ)),
            dma((ITERS,)), dma((ITERS,)),
            dma((ITERS, NY)), dma((ITERS, NY)),
            dma((ITERS, NZ)), dma((ITERS, NZ)),
            dma((ITERS,)), dma((ITERS,)),
            dma((ITERS, NX)), dma((ITERS, NX)),
            dma((ITERS, NX)), dma((ITERS, NX)),
            dma((ITERS, NX)), dma((ITERS, NX)),
            dma((7,)), dma((7,)),
            dma(()), dma((8,)),
        ],
        compiler_params=pltpu.CompilerParams(
            collective_id=0, has_side_effects=True, vmem_limit_bytes=56 * 2**20
        ),
        cost_estimate=pl.CostEstimate(flops=12884901888, bytes_accessed=8 * 2**20, transcendentals=4194304),
        name="em",
    )(minibatch, centroids)
    y = coded.reshape(2 * NX * KC, D).astype(F32)
    root = jnp.sqrt(jnp.sqrt(jnp.abs(y)))
    return (jnp.where(y < 0, -root, root), jnp.log(total).reshape(NZ * CHUNK))


def solution(mesh):
    return jax.shard_map(
        on_device,
        mesh=mesh,
        in_specs=(P(("dp", "cent"), None), P("cent", None)),
        out_specs=(P("cent", None), P("dp")),
        check_vma=False,
    )
```

```python
import functools

import jax
import jax.numpy as jnp
from jax import lax
from jax.experimental import pallas as pl
from jax.experimental.pallas import tpu as pltpu
from jax.sharding import PartitionSpec as P

MESH = pl.DeviceIdType.MESH
ITERS = 2
INV_TEMP = 20.0
PRIOR = 0.5
EPS = 1e-06
LOG2E = 1.4426950408889634
NX, NY, NZ, NC = 4, 4, 8, 2
BLOCK = 64
HALF = BLOCK // 2
CHUNK = 256
SC = 512
ROWS = NZ * SC
SPLIT = ((0, 512), (512, 256))
KC = 128
KD = NX * KC
D = 768
BF = jnp.bfloat16
F32 = jnp.float32


def encode(v):
    s = v * v
    return (v * jnp.abs(v) * s).astype(BF)


def decode(code):
    y = code.astype(F32)
    r = lax.rsqrt(jnp.maximum(jnp.abs(y), 1e-37))
    return y * (r * r * lax.rsqrt(r))


def body(
    mb, cents, out, tot_out,
    rows, cen_in, cb, c_own, expo, probs, macc, tp, ar_b, ar_c, tot, inv,
    num_own, sb, ms, rb, mr, coded, wide,
    gs, gr, cs, cr, bs, br, zs, zr, ds_, dr, rs_s, rs_r, ms_s, ms_r, ag_s, ag_r, fs, fr, loc, os_,
):
    dp, ce = lax.axis_index("dp"), lax.axis_index("cent")
    yh, x = dp // 4, lax.rem(dp, 4)
    z, yl, c = ce // 4, lax.rem(ce, 4) // 2, lax.rem(ce, 2)
    y = yh * 2 + yl

    def dev(dy=0, dx=0, dz=0, dc=0):
        yy, xx = lax.rem(y + dy + NY, NY), lax.rem(x + dx + NX, NX)
        zz, cc = lax.rem(z + dz + NZ, NZ), lax.rem(c + dc, NC)
        return ((yy // 2) * 4 + xx, zz * 4 + lax.rem(yy, 2) * 2 + cc)

    def copy(src, dst, ss, rs, to):
        return pltpu.make_async_remote_copy(
            src_ref=src, dst_ref=dst, send_sem=ss, recv_sem=rs, device_id=to, device_id_type=MESH
        )

    peers = [dict(dc=1)]
    peers += [dict(dy=d, dc=e) for d in (1, 2, 3) for e in (0, 1)]
    peers += [dict(dx=d) for d in (1, 2, 3)]
    peers += [dict(dz=d) for d in range(1, NZ)]
    barrier = pltpu.get_barrier_semaphore()
    for p in peers:
        pl.semaphore_signal(barrier, inc=1, device_id=dev(**p), device_id_type=MESH)
    load = pltpu.make_async_copy(cents.at[pl.ds(yh * KD, KD)], cen_in, loc)
    load.start()

    def unit(v):
        return v * lax.rsqrt(jnp.mean(v * v, axis=-1, keepdims=True) + EPS)

    rows[z, y, c] = unit(mb[...].astype(F32)).astype(BF)
    pl.semaphore_wait(barrier, len(peers))

    scale = INV_TEMP / D * LOG2E
    shift = INV_TEMP * LOG2E

    def score(zz, block, centers, fresh):
        s = lax.dot_general(
            centers, rows[zz].reshape(SC, D), (((1,), (1,)), ((), ())), preferred_element_type=F32
        )
        e = jnp.exp2(s * scale - shift)
        expo[zz, block] = e
        t = jnp.sum(e, axis=0, keepdims=True)
        for k in range(2):
            part = t[:, k * CHUNK : (k + 1) * CHUNK]
            tp[k, pl.ds(zz, 1)] = part if fresh else tp[k, pl.ds(zz, 1)] + part

    def blk(dy, dz, half=None):
        r = rows.at[lax.rem(z + dz + NZ, NZ), lax.rem(y + dy + NY, NY), c]
        return r if half is None else r.at[pl.ds(half * HALF, HALF)]

    def rsem(dy, dz, half=None):
        return gr.at[dy % NY, dz % NZ, half or 0]

    sent = [[], []]

    def lane(first_z, stage):
        sends = sent[0 if first_z else 1]

        def send(dy, dz, ey, ez, half=None):
            b = blk(dy, dz, half)
            copy(b, b, gs.at[len(sends)], rsem(dy - ey, dz - ez, half), dev(dy=ey, dz=ez)).start()
            sends.append((dy, dz, half))

        def landed(dy, dz, half=None):
            b = blk(dy, dz, half)
            copy(b, b, gs.at[0], rsem(dy, dz, half), dev(dc=1)).wait_recv()

        def twin(dy, dz):
            i, j = dy % NY, dz % NZ
            copy(blk(dy, dz), blk(dy, dz), cs.at[i, j], cr.at[i, j], dev(dc=1)).start()

        def along_z(dy, dz):
            if dz == 0:
                send(dy, 0, 0, 1)
                send(dy, 0, 0, -1)
            elif abs(dz) < 3:
                send(dy, dz, 0, 1 if dz < 0 else -1)
            elif abs(dz) == 3:
                send(dy, dz, 0, 1 if dz < 0 else -1, 0 if dz < 0 else 1)

        def along_y(dy, dz):
            if dy == 0:
                send(0, dz, 1, 0)
                send(0, dz, -1, 0)
            elif abs(dy) == 1:
                send(dy, dz, 1 if dy < 0 else -1, 0, 0 if dy < 0 else 1)

        def arrive(dy, dz):
            if abs(dy) == 2 and first_z or dz == 4 and (not first_z or dy == 0) or dy == 2 and dz == 0:
                landed(dy, dz, 0)
                landed(dy, dz, 1)
            else:
                landed(dy, dz)

        def group(s):
            return {0: (0,), 4: (4,)}.get(s, (-s, s)) if 0 <= s <= 4 else ()

        if first_z:
            for dz in group(stage):
                if stage:
                    arrive(0, dz)
                along_z(0, dz)
                along_y(0, dz)
                twin(0, dz)
            for dz in group(stage - 1):
                for dy in (-1, 1):
                    arrive(dy, dz)
                    along_y(dy, dz)
                    twin(dy, dz)
            for dz in group(stage - 2):
                arrive(2, dz)
                twin(2, dz)
        elif stage == 0:
            along_y(0, 0)
            along_z(0, 0)
            twin(0, 0)
        else:
            if stage == 1:
                for dy in (-1, 1, 2):
                    arrive(dy, 0)
                    along_y(dy, 0)
                    along_z(dy, 0)
                    twin(dy, 0)
            for dy in (0, -1, 1, 2):
                for dz in group(stage):
                    arrive(dy, dz)
                    along_z(dy, dz)
                    twin(dy, dz)

    for stage in range(7):

        @pl.when(c == 0)
        def _():
            lane(True, stage)

        @pl.when(c == 1)
        def _():
            lane(False, stage)

        if stage == 0:
            load.wait()
            for j in range(NX):
                cb[0, j] = unit(cen_in[pl.ds(j * KC, KC)]).astype(BF)
            c_own[...] = unit(cen_in[pl.ds(x * KC, KC)])
        if stage >= 2:
            ready = {0: (0,), 4: (4,)}.get(stage - 2, (2 - stage, stage - 2))
            for dz in ready:
                for i in range(NY):
                    his = rows.at[lax.rem(z + dz + NZ, NZ), lax.rem(y + i, NY), 1 - c]
                    copy(his, his, cs.at[i, dz % NZ], cr.at[i, dz % NZ], dev(dc=1)).wait_recv()
            for dz in ready:
                score(lax.rem(z + dz + NZ, NZ), pl.ds(0, KD), cb[0].reshape(KD, D), True)

    def all_sent(sends):
        for k, part in enumerate(sends):
            b = blk(*part)
            copy(b, b, gs.at[k], gr.at[0, 0, 0], dev(dc=1)).wait_send()

    @pl.when(c == 0)
    def _():
        all_sent(sent[0])

    @pl.when(c == 1)
    def _():
        all_sent(sent[1])

    for i in range(NY):
        for j in range(NZ):
            mine = blk(i, j)
            copy(mine, mine, cs.at[i, j], cr.at[i, j], dev(dc=1)).wait_send()

    for it in range(ITERS):
        cps = []
        if it:
            for d in (0, 1, 3, 2):
                xx = lax.rem(x + NX - d, NX)
                if d:
                    for q, (lo, n) in enumerate(SPLIT):
                        b = cb.at[it, xx, :, pl.ds(lo, n)]
                        copy(b, b, ag_s.at[q, d], ag_r.at[q, d], dev(dx=d)).wait_recv()

                def step(zz, carry):
                    score(zz, pl.ds(pl.multiple_of(xx * KC, KC), KC), cb[it, xx], d == 0)
                    return carry

                lax.fori_loop(0, NZ, step, 0, unroll=4)

        ar_b[it, y, c] = tp[c]
        for d, e in ((2, 0), (2, 1), (1, 0), (3, 0), (1, 1), (3, 1), (0, 1)):
            cps.append(
                copy(tp.at[lax.rem(c + e, 2)], ar_b.at[it, y, c], bs.at[it, d, e], br.at[it, d, e], dev(dy=d, dc=e))
            )
            cps[-1].start()
        first_sends = list(cps)
        for d, e in ((0, 1), (1, 0), (3, 0), (1, 1), (3, 1), (2, 0), (2, 1)):
            b = ar_b.at[it, lax.rem(y + NY - d, NY), lax.rem(c + e, 2)]
            copy(b, b, bs.at[it, d, e], br.at[it, d, e], dev(dy=d, dc=e)).wait_recv()
        t = ar_b[it, 0, 0] + ar_b[it, 0, 1]
        for k in range(1, NY):
            t = t + (ar_b[it, k, 0] + ar_b[it, k, 1])
        ar_c[it, z] = t
        for d in (4, 3, 5, 2, 6, 1, 7):
            cps.append(copy(ar_c.at[it, z], ar_c.at[it, z], zs.at[it, d], zr.at[it, d], dev(dz=d)))
            cps[-1].start()
        for d in (1, 7, 2, 6, 3, 5, 4):
            zz = lax.rem(z + NZ - d, NZ)
            copy(ar_c.at[it, zz], ar_c.at[it, zz], zs.at[it, d], zr.at[it, d], dev(dz=d)).wait_recv()
        t = ar_c[it, 0]
        for k in range(1, NZ):
            t = t + ar_c[it, k]
        tot[it, c] = t
        back = copy(tot.at[it, c], tot.at[it, c], ds_.at[it], dr.at[it], dev(dc=1))
        back.start()
        copy(tot.at[it, 1 - c], tot.at[it, 1 - c], ds_.at[it], dr.at[it], dev(dc=1)).wait_recv()
        inv[...] = 1.0 / tot[it]
        cps.append(back)

        def block_of(d):
            return pl.ds(pl.multiple_of(lax.rem(x + d, NX) * KC, KC), KC)

        for q, (lo, n) in enumerate(SPLIT):
            cols = pl.ds(lo, n)
            for d in (2, 1, 3, 0):
                if q == 0:
                    macc[...] = jnp.zeros_like(macc)

                    def normalise(zz, carry):
                        w = macc[...]
                        for k in range(2):
                            p = (expo[zz, block_of(d), k * CHUNK : (k + 1) * CHUNK] * inv[k, pl.ds(zz, 1)]).astype(BF)
                            probs[block_of(d), pl.ds(pl.multiple_of(zz * SC + k * CHUNK, CHUNK), CHUNK)] = p
                            p = p.astype(F32)
                            w = w + (p[:, :128] + p[:, 128:])
                        macc[...] = w
                        return carry

                    lax.fori_loop(0, NZ, normalise, 0, unroll=4)
                num = lax.dot_general(
                    probs[block_of(d)], rows[:, :, :, :, cols].reshape(ROWS, n), (((1,), (0,)), ((), ())),
                    preferred_element_type=F32,
                )
                if d:
                    sb[it, d - 1, :, cols] = encode(num)
                    b = (it, d - 1, slice(None), cols)
                    cps.append(copy(sb.at[b], rb.at[b], rs_s.at[it, q, d], rs_r.at[it, q, d], dev(dx=d)))
                    cps[-1].start()
                else:
                    num_own[:, cols] = num
                if q == 0:
                    mass = jnp.sum(macc[...], axis=1, keepdims=True)
                    if d:
                        ms[it, d - 1] = jnp.broadcast_to(mass, (KC, 128)).T[:8]
                        cps.append(copy(ms.at[it, d - 1], mr.at[it, d - 1], ms_s.at[it, d], ms_r.at[it, d], dev(dx=d)))
                        cps[-1].start()

        final = it == ITERS - 1
        if final:

            def slot(other, d, q):
                lo, n = SPLIT[q]
                return (1 - yh if other else yh, lax.rem(x + d + NX, NX), slice(None), pl.ds(lo, n))

            def go(other, d, k, q, **to):
                b = coded.at[slot(other, d, q)]
                cps.append(copy(b, b, fs.at[q, k], fr.at[q, k], dev(**to)))
                cps[-1].start()

            def come(other, d, k, q):
                b = coded.at[slot(other, d, q)]
                copy(b, b, fs.at[q, k], fr.at[q, k], dev(dc=1)).wait_recv()

            stores = []

            def store(other, d, q):
                b = slot(other, d, q)
                wide[b] = decode(coded[b])
                stores.append(pltpu.make_async_copy(wide.at[b], out.at[b], os_.at[len(stores)]))
                stores[-1].start()

        for q, (lo, n) in enumerate(SPLIT):
            cols = pl.ds(lo, n)
            if q == 0:
                rowm = jnp.zeros((8, 128), F32)
                for d in (1, 3, 2):
                    copy(ms.at[it, d - 1], mr.at[it, d - 1], ms_s.at[it, d], ms_r.at[it, d], dev(dx=d)).wait_recv()
                    rowm = rowm + mr[it, d - 1]
                share = 1.0 / (mass + jnp.broadcast_to(rowm[:1], (KC, 128)).T[:, :1] + PRIOR)
            num = num_own[:, cols] + PRIOR * c_own[:, cols]
            for d in (1, 3, 2):
                b = (it, d - 1, slice(None), cols)
                copy(sb.at[b], rb.at[b], rs_s.at[it, q, d], rs_r.at[it, q, d], dev(dx=d)).wait_recv()
                num = num + decode(rb[b])
            new = num * share
            if not final:
                c_own[:, cols] = new
                cb[it + 1, x, :, cols] = new.astype(BF)
                for d in (1, 3, 2):
                    b = cb.at[it + 1, x, :, cols]
                    cps.append(copy(b, b, ag_s.at[q, d], ag_r.at[q, d], dev(dx=d)))
                    cps[-1].start()
            else:
                coded[slot(False, 0, q)] = encode(new)
                go(False, 0, 0, q, dy=2)
                go(False, 0, 1, q, dx=1)
                go(False, 0, 2, q, dx=-1)
                go(False, 0, 3, q, dx=2)

        if final:
            logs = jnp.log(tot[it, yh])
            for k in range(2):
                tot_out[pl.ds(k, NZ, 2)] = logs[:, k * 128 : (k + 1) * 128]
            for q in range(2):
                store(False, 0, q)
            for q in range(2):
                come(False, 1, 2, q)
                go(False, 1, 4, q, dy=2)
                come(True, 0, 0, q)
                go(True, 0, 5, q, dx=1)
                store(False, 1, q)
                store(True, 0, q)
            for q in range(2):
                come(False, -1, 1, q)
                store(False, -1, q)
                come(True, 1, 4, q)
                go(True, 1, 6, q, dx=-1)
                store(True, 1, q)
            for q in range(2):
                come(False, 2, 3, q)
                store(False, 2, q)
                come(True, -1, 5, q)
                store(True, -1, q)
            for q in range(2):
                come(True, 2, 6, q)
                store(True, 2, q)
            for st in stores:
                st.wait()
        for cp in cps:
            cp.wait_send()


def on_device(minibatch, centroids):
    dma = pltpu.SemaphoreType.DMA
    refined, logs = pl.pallas_call(
        body,
        out_shape=(
            jax.ShapeDtypeStruct((2, NX, KC, D), F32),
            jax.ShapeDtypeStruct((2 * NZ, 128), F32),
        ),
        in_specs=[pl.BlockSpec(memory_space=pltpu.VMEM), pl.BlockSpec(memory_space=pl.ANY)],
        out_specs=(pl.BlockSpec(memory_space=pl.ANY), pl.BlockSpec(memory_space=pltpu.VMEM)),
        scratch_shapes=[
            pltpu.VMEM((NZ, NY, NC, BLOCK, D), BF),
            pltpu.VMEM((KD, D), F32),
            pltpu.VMEM((ITERS, NX, KC, D), BF),
            pltpu.VMEM((KC, D), F32),
            pltpu.VMEM((NZ, KD, SC), F32),
            pltpu.VMEM((KD, ROWS), BF),
            pltpu.VMEM((KC, 128), F32),
            pltpu.VMEM((2, NZ, CHUNK), F32),
            pltpu.VMEM((ITERS, NY, NC, NZ, CHUNK), F32),
            pltpu.VMEM((ITERS, NZ, NZ, CHUNK), F32),
            pltpu.VMEM((ITERS, 2, NZ, CHUNK), F32),
            pltpu.VMEM((2, NZ, CHUNK), F32),
            pltpu.VMEM((KC, D), F32),
            pltpu.VMEM((ITERS, 3, KC, D), BF),
            pltpu.VMEM((ITERS, 3, 8, 128), F32),
            pltpu.VMEM((ITERS, 3, KC, D), BF),
            pltpu.VMEM((ITERS, 3, 8, 128), F32),
            pltpu.VMEM((2, NX, KC, D), BF),
            pltpu.VMEM((2, NX, KC, D), F32),
            dma((40,)), dma((NY, NZ, 2)),
            dma((NY, NZ)), dma((NY, NZ)),
            dma((ITERS, NY, NC)), dma((ITERS, NY, NC)),
            dma((ITERS, NZ)), dma((ITERS, NZ)),
            dma((ITERS,)), dma((ITERS,)),
            dma((ITERS, 2, NX)), dma((ITERS, 2, NX)),
            dma((ITERS, NX)), dma((ITERS, NX)),
            dma((2, NX)), dma((2, NX)),
            dma((2, 7)), dma((2, 7)),
            dma(()), dma((16,)),
        ],
        compiler_params=pltpu.CompilerParams(
            collective_id=0, has_side_effects=True, vmem_limit_bytes=56 * 2**20
        ),
        cost_estimate=pl.CostEstimate(flops=12884901888, bytes_accessed=8 * 2**20, transcendentals=4194304),
        name="em",
    )(minibatch, centroids)
    return (refined.reshape(2 * NX * KC, D), logs.reshape(NZ * CHUNK))


def solution(mesh):
    return jax.shard_map(
        on_device,
        mesh=mesh,
        in_specs=(P(("dp", "cent"), None), P("cent", None)),
        out_specs=(P("cent", None), P("dp")),
        check_vma=False,
    )
```

```python
import functools

import jax
import jax.numpy as jnp
from jax import lax
from jax.experimental import pallas as pl
from jax.experimental.pallas import tpu as pltpu
from jax.sharding import PartitionSpec as P

MESH = pl.DeviceIdType.MESH
ITERS = 2
INV_TEMP = 20.0
PRIOR = 0.5
EPS = 1e-06
LOG2E = 1.4426950408889634
NX, NY, NZ, NC = 4, 4, 8, 2
BLOCK = 64
HALF = BLOCK // 2
CHUNK = 256
SC = 512
ROWS = NZ * SC
SPLIT = ((0, 512), (512, 256))
KC = 128
KD = NX * KC
D = 768
BF = jnp.bfloat16
F32 = jnp.float32


def encode(v):
    s = v * v
    return (v * jnp.abs(v) * s).astype(BF)


def decode(code):
    y = code.astype(F32)
    r = lax.rsqrt(jnp.maximum(jnp.abs(y), 1e-37))
    return y * (r * r * lax.rsqrt(r))


def body(
    mb, cents, out, tot_out,
    rows, cen_in, cb, c_own, expo, probs, macc, tp, ar_b, ar_c, tot, inv,
    num_own, sb, ms, rb, mr, coded, wide,
    gs, gr, cs, cr, bs, br, zs, zr, ds_, dr, rs_s, rs_r, ms_s, ms_r, ag_s, ag_r, fs, fr, loc, os_,
):
    dp, ce = lax.axis_index("dp"), lax.axis_index("cent")
    yh, x = dp // 4, lax.rem(dp, 4)
    z, yl, c = ce // 4, lax.rem(ce, 4) // 2, lax.rem(ce, 2)
    y = yh * 2 + yl

    def dev(dy=0, dx=0, dz=0, dc=0):
        yy, xx = lax.rem(y + dy + NY, NY), lax.rem(x + dx + NX, NX)
        zz, cc = lax.rem(z + dz + NZ, NZ), lax.rem(c + dc, NC)
        return ((yy // 2) * 4 + xx, zz * 4 + lax.rem(yy, 2) * 2 + cc)

    def copy(src, dst, ss, rs, to):
        return pltpu.make_async_remote_copy(
            src_ref=src, dst_ref=dst, send_sem=ss, recv_sem=rs, device_id=to, device_id_type=MESH
        )

    peers = [dict(dc=1)]
    peers += [dict(dy=d) for d in (1, 3)]
    peers += [dict(dx=d) for d in (1, 2, 3)]
    peers += [dict(dz=d) for d in (1, NZ - 1)]
    barrier = pltpu.get_barrier_semaphore()
    for p in peers:
        pl.semaphore_signal(barrier, inc=1, device_id=dev(**p), device_id_type=MESH)
    load = pltpu.make_async_copy(cents.at[pl.ds(yh * KD, KD)], cen_in, loc)
    load.start()

    def unit(v):
        return v * lax.rsqrt(jnp.mean(v * v, axis=-1, keepdims=True) + EPS)

    rows[z, y, c] = unit(mb[...].astype(F32)).astype(BF)
    pl.semaphore_wait(barrier, len(peers))

    scale = INV_TEMP / D * LOG2E
    shift = INV_TEMP * LOG2E

    def score(zz, block, centers, fresh):
        s = lax.dot_general(
            centers, rows[zz].reshape(SC, D), (((1,), (1,)), ((), ())), preferred_element_type=F32
        )
        e = jnp.exp2(s * scale - shift)
        expo[zz, block] = e
        t = jnp.sum(e, axis=0, keepdims=True)
        for k in range(2):
            part = t[:, k * CHUNK : (k + 1) * CHUNK]
            tp[k, pl.ds(zz, 1)] = part if fresh else tp[k, pl.ds(zz, 1)] + part

    def blk(dy, dz, half=None):
        r = rows.at[lax.rem(z + dz + NZ, NZ), lax.rem(y + dy + NY, NY), c]
        return r if half is None else r.at[pl.ds(half * HALF, HALF)]

    def rsem(dy, dz, half=None):
        return gr.at[dy % NY, dz % NZ, half or 0]

    sent = [[], []]

    def lane(first_z, stage):
        sends = sent[0 if first_z else 1]

        def send(dy, dz, ey, ez, half=None):
            b = blk(dy, dz, half)
            copy(b, b, gs.at[len(sends)], rsem(dy - ey, dz - ez, half), dev(dy=ey, dz=ez)).start()
            sends.append((dy, dz, half))

        def landed(dy, dz, half=None):
            b = blk(dy, dz, half)
            copy(b, b, gs.at[0], rsem(dy, dz, half), dev(dc=1)).wait_recv()

        def twin(dy, dz):
            i, j = dy % NY, dz % NZ
            copy(blk(dy, dz), blk(dy, dz), cs.at[i, j], cr.at[i, j], dev(dc=1)).start()

        def along_z(dy, dz):
            if dz == 0:
                send(dy, 0, 0, 1)
                send(dy, 0, 0, -1)
            elif abs(dz) < 3:
                send(dy, dz, 0, 1 if dz < 0 else -1)
            elif abs(dz) == 3:
                send(dy, dz, 0, 1 if dz < 0 else -1, 0 if dz < 0 else 1)

        def along_y(dy, dz):
            if dy == 0:
                send(0, dz, 1, 0)
                send(0, dz, -1, 0)
            elif abs(dy) == 1:
                send(dy, dz, 1 if dy < 0 else -1, 0, 0 if dy < 0 else 1)

        def arrive(dy, dz):
            if abs(dy) == 2 and first_z or dz == 4 and (not first_z or dy == 0) or dy == 2 and dz == 0:
                landed(dy, dz, 0)
                landed(dy, dz, 1)
            else:
                landed(dy, dz)

        if first_z:
            for dz in group(stage):
                if stage:
                    arrive(0, dz)
                along_z(0, dz)
                along_y(0, dz)
                twin(0, dz)
            for dz in group(stage - 1):
                for dy in (-1, 1):
                    arrive(dy, dz)
                    along_y(dy, dz)
                    twin(dy, dz)
            for dz in group(stage - 2):
                arrive(2, dz)
                twin(2, dz)
        elif stage == 0:
            along_y(0, 0)
            along_z(0, 0)
            twin(0, 0)
        else:
            if stage == 1:
                for dy in (-1, 1, 2):
                    arrive(dy, 0)
                    along_y(dy, 0)
                    along_z(dy, 0)
                    twin(dy, 0)
            for dy in (0, -1, 1, 2):
                for dz in group(stage):
                    arrive(dy, dz)
                    along_z(dy, dz)
                    twin(dy, dz)

    def group(s):
        return {0: (0,), 4: (4,)}.get(s, (-s, s)) if 0 <= s <= 4 else ()

    def score_group(s):
        for dz in group(s):
            for i in range(NY):
                his = rows.at[lax.rem(z + dz + NZ, NZ), lax.rem(y + i, NY), 1 - c]
                copy(his, his, cs.at[i, dz % NZ], cr.at[i, dz % NZ], dev(dc=1)).wait_recv()
        for dz in group(s):
            score(lax.rem(z + dz + NZ, NZ), pl.ds(0, KD), cb[0].reshape(KD, D), True)

    for stage in range(7):

        @pl.when(c == 0)
        def _():
            lane(True, stage)

        @pl.when(c == 1)
        def _():
            lane(False, stage)

        if stage == 0:
            load.wait()
            for d in range(NX):
                first = pl.multiple_of(lax.rem(x + NX - d, NX) * KC, KC)
                v = unit(cen_in[pl.ds(first, KC)])
                cb[0, d] = v.astype(BF)
                if d == 0:
                    c_own[...] = v
        score_group(stage - 2)

    def all_sent(sends):
        for k, part in enumerate(sends):
            b = blk(*part)
            copy(b, b, gs.at[k], gr.at[0, 0, 0], dev(dc=1)).wait_send()

    @pl.when(c == 0)
    def _():
        all_sent(sent[0])

    @pl.when(c == 1)
    def _():
        all_sent(sent[1])

    for i in range(NY):
        for j in range(NZ):
            mine = blk(i, j)
            copy(mine, mine, cs.at[i, j], cr.at[i, j], dev(dc=1)).wait_send()

    for it in range(ITERS):
        cps = []
        if it:
            def own(zz, carry):
                score(zz, pl.ds(0, KC), cb[it, 0], True)
                return carry

            def others(zz, carry):
                score(zz, pl.ds(KC, KD - KC), cb[it, 1:].reshape(KD - KC, D), False)
                return carry

            lax.fori_loop(0, NZ, own, 0, unroll=4)
            relays = []
            for q, (lo, n) in enumerate(SPLIT):
                cols = pl.ds(lo, n)
                for d, k, half in ((1, 2, 0), (3, 0, 1)):
                    b = cb.at[it, d, :, cols]
                    copy(b, b, ag_s.at[q, d], ag_r.at[q, d], dev(dx=d)).wait_recv()
                    part = pl.ds(half * KC // 2, KC // 2)
                    src, dst = cb.at[it, d, part, cols], cb.at[it, 2, part, cols]
                    relays.append(copy(src, dst, ag_s.at[q, k], ag_r.at[q, k], dev(dx=d)))
                    relays[-1].start()
            for r in relays:
                r.wait_recv()
            cps += relays
            lax.fori_loop(0, NZ, others, 0, unroll=4)

        ar_b[it, y, c] = tp[c]
        for d, e in ((2, 0), (2, 1), (1, 0), (3, 0), (1, 1), (3, 1), (0, 1)):
            cps.append(
                copy(tp.at[lax.rem(c + e, 2)], ar_b.at[it, y, c], bs.at[it, d, e], br.at[it, d, e], dev(dy=d, dc=e))
            )
            cps[-1].start()
        first_sends = list(cps)
        for d, e in ((0, 1), (1, 0), (3, 0), (1, 1), (3, 1), (2, 0), (2, 1)):
            b = ar_b.at[it, lax.rem(y + NY - d, NY), lax.rem(c + e, 2)]
            copy(b, b, bs.at[it, d, e], br.at[it, d, e], dev(dy=d, dc=e)).wait_recv()
        t = ar_b[it, 0, 0] + ar_b[it, 0, 1]
        for k in range(1, NY):
            t = t + (ar_b[it, k, 0] + ar_b[it, k, 1])
        ar_c[it, z] = t
        for d in (4, 3, 5, 2, 6, 1, 7):
            cps.append(copy(ar_c.at[it, z], ar_c.at[it, z], zs.at[it, d], zr.at[it, d], dev(dz=d)))
            cps[-1].start()
        for d in (1, 7, 2, 6, 3, 5, 4):
            zz = lax.rem(z + NZ - d, NZ)
            copy(ar_c.at[it, zz], ar_c.at[it, zz], zs.at[it, d], zr.at[it, d], dev(dz=d)).wait_recv()
        t = ar_c[it, 0]
        for k in range(1, NZ):
            t = t + ar_c[it, k]
        tot[it, c] = t
        back = copy(tot.at[it, c], tot.at[it, c], ds_.at[it], dr.at[it], dev(dc=1))
        back.start()
        copy(tot.at[it, 1 - c], tot.at[it, 1 - c], ds_.at[it], dr.at[it], dev(dc=1)).wait_recv()
        inv[...] = 1.0 / tot[it]
        cps.append(back)

        def block_of(d):
            return pl.ds((NX - d) % NX * KC, KC)

        for q, (lo, n) in enumerate(SPLIT):
            cols = pl.ds(lo, n)
            for d in (2, 1, 3, 0):
                if q == 0:
                    macc[...] = jnp.zeros_like(macc)

                    def normalise(zz, carry):
                        w = macc[...]
                        for k in range(2):
                            p = (expo[zz, block_of(d), k * CHUNK : (k + 1) * CHUNK] * inv[k, pl.ds(zz, 1)]).astype(BF)
                            probs[block_of(d), pl.ds(pl.multiple_of(zz * SC + k * CHUNK, CHUNK), CHUNK)] = p
                            p = p.astype(F32)
                            w = w + (p[:, :128] + p[:, 128:])
                        macc[...] = w
                        return carry

                    lax.fori_loop(0, NZ, normalise, 0, unroll=4)
                num = lax.dot_general(
                    probs[block_of(d)], rows[:, :, :, :, cols].reshape(ROWS, n), (((1,), (0,)), ((), ())),
                    preferred_element_type=F32,
                )
                if d:
                    sb[it, d - 1, :, cols] = encode(num)
                    b = (it, d - 1, slice(None), cols)
                    cps.append(copy(sb.at[b], rb.at[b], rs_s.at[it, q, d], rs_r.at[it, q, d], dev(dx=d)))
                    cps[-1].start()
                else:
                    num_own[:, cols] = num
                if q == 0:
                    mass = jnp.sum(macc[...], axis=1, keepdims=True)
                    if d:
                        ms[it, d - 1] = jnp.broadcast_to(mass, (KC, 128)).T[:8]
                        cps.append(copy(ms.at[it, d - 1], mr.at[it, d - 1], ms_s.at[it, d], ms_r.at[it, d], dev(dx=d)))
                        cps[-1].start()

        final = it == ITERS - 1
        if final:

            def slot(other, d, q, half=None):
                part = slice(None) if half is None else pl.ds(half * KC // 2, KC // 2)
                return (1 - yh if other else yh, lax.rem(x + d + NX, NX), part, pl.ds(*SPLIT[q]))

            def go(other, d, k, q, half=None, **to):
                b = coded.at[slot(other, d, q, half)]
                cps.append(copy(b, b, fs.at[q, k], fr.at[q, k], dev(**to)))
                cps[-1].start()

            def come(other, d, k, q, half=None):
                b = coded.at[slot(other, d, q, half)]
                copy(b, b, fs.at[q, k], fr.at[q, k], dev(dc=1)).wait_recv()

            stores = []

            def store(other, d, q):
                b = slot(other, d, q)
                wide[b] = decode(coded[b])
                stores.append(pltpu.make_async_copy(wide.at[b], out.at[b], os_.at[len(stores)]))
                stores[-1].start()

        for q, (lo, n) in enumerate(SPLIT):
            cols = pl.ds(lo, n)
            if q == 0:
                rowm = jnp.zeros((8, 128), F32)
                for d in (1, 3, 2):
                    copy(ms.at[it, d - 1], mr.at[it, d - 1], ms_s.at[it, d], ms_r.at[it, d], dev(dx=d)).wait_recv()
                    rowm = rowm + mr[it, d - 1]
                share = 1.0 / (mass + jnp.broadcast_to(rowm[:1], (KC, 128)).T[:, :1] + PRIOR)
            num = num_own[:, cols] + PRIOR * c_own[:, cols]
            for d in (1, 3, 2):
                b = (it, d - 1, slice(None), cols)
                copy(sb.at[b], rb.at[b], rs_s.at[it, q, d], rs_r.at[it, q, d], dev(dx=d)).wait_recv()
                num = num + decode(rb[b])
            new = num * share
            if not final:
                c_own[:, cols] = new
                cb[it + 1, 0, :, cols] = new.astype(BF)
                for d in (1, 3):
                    b = cb.at[it + 1, 0, :, cols]
                    cps.append(copy(b, cb.at[it + 1, d, :, cols], ag_s.at[q, d], ag_r.at[q, d], dev(dx=d)))
                    cps[-1].start()
            else:
                coded[slot(False, 0, q)] = encode(new)
                go(False, 0, 0, q, dy=2)
                go(False, 0, 1, q, dx=1)
                go(False, 0, 2, q, dx=-1)

        if final:
            logs = jnp.log(tot[it, yh])
            for k in range(2):
                tot_out[pl.ds(k, NZ, 2)] = logs[:, k * 128 : (k + 1) * 128]
            for q in range(len(SPLIT)):
                store(False, 0, q)
            for q in range(len(SPLIT)):
                come(False, 1, 2, q)
                go(False, 1, 4, q, dy=2)
                go(False, 1, 7, q, 1, dx=-1)
                come(False, -1, 1, q)
                go(False, -1, 3, q, 0, dx=1)
                come(True, 0, 0, q)
                go(True, 0, 5, q, dx=1)
                store(False, 1, q)
                store(False, -1, q)
            for q in range(len(SPLIT)):
                come(True, 1, 4, q)
                go(True, 1, 6, q, dx=-1)
                store(True, 0, q)
                store(True, 1, q)
            for q in range(len(SPLIT)):
                come(False, 2, 3, q, 0)
                come(False, 2, 7, q, 1)
                store(False, 2, q)
                come(True, -1, 5, q)
                store(True, -1, q)
            for q in range(len(SPLIT)):
                come(True, 2, 6, q)
                store(True, 2, q)
            for st in stores:
                st.wait()
        for cp in cps:
            cp.wait_send()


def hand_on(refined, logs, refined_out, logs_out, held, held_logs, sems):
    parts = [(logs, held_logs, logs_out)]
    parts += [(refined.at[k], held.at[k], refined_out.at[k]) for k in range(2 * NX)]
    into = [pltpu.make_async_copy(a, b, sems.at[0, k]) for k, (a, b, _) in enumerate(parts)]
    back = [pltpu.make_async_copy(b, o, sems.at[1, k]) for k, (_, b, o) in enumerate(parts)]
    for cp in into:
        cp.start()
    for i, o in zip(into, back):
        i.wait()
        o.start()
    for cp in back:
        cp.wait()


def on_device(minibatch, centroids):
    dma = pltpu.SemaphoreType.DMA
    refined, logs = pl.pallas_call(
        body,
        out_shape=(
            jax.ShapeDtypeStruct((2, NX, KC, D), F32),
            jax.ShapeDtypeStruct((2 * NZ, 128), F32),
        ),
        in_specs=[pl.BlockSpec(memory_space=pltpu.VMEM), pl.BlockSpec(memory_space=pl.ANY)],
        out_specs=(pl.BlockSpec(memory_space=pl.ANY), pl.BlockSpec(memory_space=pltpu.VMEM)),
        scratch_shapes=[
            pltpu.VMEM((NZ, NY, NC, BLOCK, D), BF),
            pltpu.VMEM((KD, D), F32),
            pltpu.VMEM((ITERS, NX, KC, D), BF),
            pltpu.VMEM((KC, D), F32),
            pltpu.VMEM((NZ, KD, SC), F32),
            pltpu.VMEM((KD, ROWS), BF),
            pltpu.VMEM((KC, 128), F32),
            pltpu.VMEM((2, NZ, CHUNK), F32),
            pltpu.VMEM((ITERS, NY, NC, NZ, CHUNK), F32),
            pltpu.VMEM((ITERS, NZ, NZ, CHUNK), F32),
            pltpu.VMEM((ITERS, 2, NZ, CHUNK), F32),
            pltpu.VMEM((2, NZ, CHUNK), F32),
            pltpu.VMEM((KC, D), F32),
            pltpu.VMEM((ITERS, 3, KC, D), BF),
            pltpu.VMEM((ITERS, 3, 8, 128), F32),
            pltpu.VMEM((ITERS, 3, KC, D), BF),
            pltpu.VMEM((ITERS, 3, 8, 128), F32),
            pltpu.VMEM((2, NX, KC, D), BF),
            pltpu.VMEM((2, NX, KC, D), F32),
            dma((40,)), dma((NY, NZ, 2)),
            dma((NY, NZ)), dma((NY, NZ)),
            dma((ITERS, NY, NC)), dma((ITERS, NY, NC)),
            dma((ITERS, NZ)), dma((ITERS, NZ)),
            dma((ITERS,)), dma((ITERS,)),
            dma((ITERS, len(SPLIT), NX)), dma((ITERS, len(SPLIT), NX)),
            dma((ITERS, NX)), dma((ITERS, NX)),
            dma((len(SPLIT), NX)), dma((len(SPLIT), NX)),
            dma((len(SPLIT), 8)), dma((len(SPLIT), 8)),
            dma(()), dma((8 * len(SPLIT),)),
        ],
        compiler_params=pltpu.CompilerParams(
            collective_id=0, has_side_effects=True, vmem_limit_bytes=56 * 2**20
        ),
        cost_estimate=pl.CostEstimate(flops=12884901888, bytes_accessed=8 * 2**20, transcendentals=4194304),
        name="em",
    )(minibatch, centroids)
    n = 2 * NX
    refined, logs = pl.pallas_call(
        hand_on,
        out_shape=(jax.ShapeDtypeStruct((n, KC, D), F32), jax.ShapeDtypeStruct((2 * NZ, 128), F32)),
        in_specs=[pl.BlockSpec(memory_space=pl.ANY)] * 2,
        out_specs=[pl.BlockSpec(memory_space=pl.ANY)] * 2,
        scratch_shapes=[
            pltpu.VMEM((n, KC, D), F32),
            pltpu.VMEM((2 * NZ, 128), F32),
            dma((2, n + 1)),
        ],
        name="hand_on",
    )(refined.reshape(n, KC, D), logs)
    return (refined.reshape(n * KC, D), logs.reshape(NZ * CHUNK))


def solution(mesh):
    return jax.shard_map(
        on_device,
        mesh=mesh,
        in_specs=(P(("dp", "cent"), None), P("cent", None)),
        out_specs=(P("cent", None), P("dp")),
        check_vma=False,
    )
```

```python
import functools

import jax
import jax.numpy as jnp
from jax import lax
from jax.experimental import pallas as pl
from jax.experimental.pallas import tpu as pltpu
from jax.sharding import PartitionSpec as P

MESH = pl.DeviceIdType.MESH
ITERS = 2
INV_TEMP = 20.0
PRIOR = 0.5
EPS = 1e-06
LOG2E = 1.4426950408889634
NX, NY, NZ, NC = 4, 4, 8, 2
BLOCK = 64
HALF = BLOCK // 2
CHUNK = 256
SC = 512
ROWS = NZ * SC
SLOT = {0: 0, 1: 1, 3: 2, 2: 3}
SPLIT = ((0, 384), (384, 384))
KC = 128
KD = NX * KC
D = 768
BF = jnp.bfloat16
F32 = jnp.float32


def encode(v):
    s = v * v
    return (v * jnp.abs(v) * s).astype(BF)


def decode(code):
    y = code.astype(F32)
    r = lax.rsqrt(jnp.maximum(jnp.abs(y), 1e-37))
    return y * (r * r * lax.rsqrt(r))


def body(
    mb, cents, out, tot_out,
    rows, cen_in, cb, c_own, expo, probs, macc, tp, ar_b, ar_c, tot, inv,
    num_own, sb, ms, rb, mr, coded, wide,
    gs, gr, cs, cr, bs, br, zs, zr, ds_, dr, rs_s, rs_r, ms_s, ms_r, ag_s, ag_r, fs, fr, loc, os_,
):
    dp, ce = lax.axis_index("dp"), lax.axis_index("cent")
    yh, x = dp // 4, lax.rem(dp, 4)
    z, yl, c = ce // 4, lax.rem(ce, 4) // 2, lax.rem(ce, 2)
    y = yh * 2 + yl

    def dev(dy=0, dx=0, dz=0, dc=0):
        yy, xx = lax.rem(y + dy + NY, NY), lax.rem(x + dx + NX, NX)
        zz, cc = lax.rem(z + dz + NZ, NZ), lax.rem(c + dc, NC)
        return ((yy // 2) * 4 + xx, zz * 4 + lax.rem(yy, 2) * 2 + cc)

    def copy(src, dst, ss, rs, to):
        return pltpu.make_async_remote_copy(
            src_ref=src, dst_ref=dst, send_sem=ss, recv_sem=rs, device_id=to, device_id_type=MESH
        )

    peers = [dict(dc=1)]
    peers += [dict(dy=d) for d in (1, 3)]
    peers += [dict(dx=d) for d in (1, 2, 3)]
    peers += [dict(dz=d) for d in (1, NZ - 1)]
    barrier = pltpu.get_barrier_semaphore()
    for p in peers:
        pl.semaphore_signal(barrier, inc=1, device_id=dev(**p), device_id_type=MESH)
    load = pltpu.make_async_copy(cents.at[pl.ds(yh * KD, KD)], cen_in, loc)
    load.start()

    def unit(v):
        return v * lax.rsqrt(jnp.mean(v * v, axis=-1, keepdims=True) + EPS)

    rows[z, y, c] = unit(mb[...].astype(F32)).astype(BF)
    pl.semaphore_wait(barrier, len(peers))

    scale = INV_TEMP / D * LOG2E
    shift = INV_TEMP * LOG2E

    def score(zz, block, centers, fresh):
        s = lax.dot_general(
            centers, rows[zz].reshape(SC, D), (((1,), (1,)), ((), ())), preferred_element_type=F32
        )
        e = jnp.exp2(s * scale - shift)
        expo[zz, block] = e
        t = jnp.sum(e, axis=0, keepdims=True)
        for k in range(2):
            part = t[:, k * CHUNK : (k + 1) * CHUNK]
            tp[k, pl.ds(zz, 1)] = part if fresh else tp[k, pl.ds(zz, 1)] + part

    def blk(dy, dz, half=None):
        r = rows.at[lax.rem(z + dz + NZ, NZ), lax.rem(y + dy + NY, NY), c]
        return r if half is None else r.at[pl.ds(half * HALF, HALF)]

    def rsem(dy, dz, half=None):
        return gr.at[dy % NY, dz % NZ, half or 0]

    sent = [[], []]

    def lane(first_z, stage):
        sends = sent[0 if first_z else 1]

        def send(dy, dz, ey, ez, half=None):
            b = blk(dy, dz, half)
            copy(b, b, gs.at[len(sends)], rsem(dy - ey, dz - ez, half), dev(dy=ey, dz=ez)).start()
            sends.append((dy, dz, half))

        def landed(dy, dz, half=None):
            b = blk(dy, dz, half)
            copy(b, b, gs.at[0], rsem(dy, dz, half), dev(dc=1)).wait_recv()

        def twin(dy, dz):
            i, j = dy % NY, dz % NZ
            copy(blk(dy, dz), blk(dy, dz), cs.at[i, j], cr.at[i, j], dev(dc=1)).start()

        def along_z(dy, dz):
            if dz == 0:
                send(dy, 0, 0, 1)
                send(dy, 0, 0, -1)
            elif abs(dz) < 3:
                send(dy, dz, 0, 1 if dz < 0 else -1)
            elif abs(dz) == 3:
                send(dy, dz, 0, 1 if dz < 0 else -1, 0 if dz < 0 else 1)

        def along_y(dy, dz):
            if dy == 0:
                send(0, dz, 1, 0)
                send(0, dz, -1, 0)
            elif abs(dy) == 1:
                send(dy, dz, 1 if dy < 0 else -1, 0, 0 if dy < 0 else 1)

        def arrive(dy, dz):
            if abs(dy) == 2 and first_z or dz == 4 and (not first_z or dy == 0) or dy == 2 and dz == 0:
                landed(dy, dz, 0)
                landed(dy, dz, 1)
            else:
                landed(dy, dz)

        if first_z:
            for dz in group(stage):
                if stage:
                    arrive(0, dz)
                along_z(0, dz)
                along_y(0, dz)
                twin(0, dz)
            for dz in group(stage - 1):
                for dy in (-1, 1):
                    arrive(dy, dz)
                    along_y(dy, dz)
                    twin(dy, dz)
            for dz in group(stage - 2):
                arrive(2, dz)
                twin(2, dz)
        elif stage == 0:
            along_y(0, 0)
            along_z(0, 0)
            twin(0, 0)
        else:
            if stage == 1:
                for dy in (-1, 1, 2):
                    arrive(dy, 0)
                    along_y(dy, 0)
                    along_z(dy, 0)
                    twin(dy, 0)
            for dy in (0, -1, 1, 2):
                for dz in group(stage):
                    arrive(dy, dz)
                    along_z(dy, dz)
                    twin(dy, dz)

    def group(s):
        return {0: (0,), 4: (4,)}.get(s, (-s, s)) if 0 <= s <= 4 else ()

    def score_group(s):
        for dz in group(s):
            for i in range(NY):
                his = rows.at[lax.rem(z + dz + NZ, NZ), lax.rem(y + i, NY), 1 - c]
                copy(his, his, cs.at[i, dz % NZ], cr.at[i, dz % NZ], dev(dc=1)).wait_recv()
        for dz in group(s):
            score(lax.rem(z + dz + NZ, NZ), pl.ds(0, KD), cb[0].reshape(KD, D), True)

    for stage in range(7):

        @pl.when(c == 0)
        def _():
            lane(True, stage)

        @pl.when(c == 1)
        def _():
            lane(False, stage)

        if stage == 0:
            load.wait()
            for d in range(NX):
                first = pl.multiple_of(lax.rem(x + NX - d, NX) * KC, KC)
                v = unit(cen_in[pl.ds(first, KC)])
                cb[0, SLOT[d]] = v.astype(BF)
                if d == 0:
                    c_own[...] = v
        score_group(stage - 2)

    def all_sent(sends):
        for k, part in enumerate(sends):
            b = blk(*part)
            copy(b, b, gs.at[k], gr.at[0, 0, 0], dev(dc=1)).wait_send()

    @pl.when(c == 0)
    def _():
        all_sent(sent[0])

    @pl.when(c == 1)
    def _():
        all_sent(sent[1])

    for i in range(NY):
        for j in range(NZ):
            mine = blk(i, j)
            copy(mine, mine, cs.at[i, j], cr.at[i, j], dev(dc=1)).wait_send()

    for it in range(ITERS):
        cps = []
        if it:
            def own(zz, carry):
                score(zz, pl.ds(0, KC), cb[it, 0], True)
                return carry

            def near(zz, carry):
                score(zz, pl.ds(KC, 2 * KC), cb[it, 1:3].reshape(2 * KC, D), False)
                return carry

            def far(zz, carry):
                score(zz, pl.ds(3 * KC, KC), cb[it, 3], False)
                return carry

            lax.fori_loop(0, NZ, own, 0, unroll=4)
            relays = []
            for q, (lo, n) in enumerate(SPLIT):
                cols = pl.ds(lo, n)
                for d, k, half in ((1, 2, 0), (3, 0, 1)):
                    b = cb.at[it, SLOT[d], :, cols]
                    copy(b, b, ag_s.at[q, d], ag_r.at[q, d], dev(dx=d)).wait_recv()
                    part = pl.ds(half * KC // 2, KC // 2)
                    src, dst = cb.at[it, SLOT[d], part, cols], cb.at[it, SLOT[2], part, cols]
                    relays.append(copy(src, dst, ag_s.at[q, k], ag_r.at[q, k], dev(dx=d)))
                    relays[-1].start()
            lax.fori_loop(0, NZ, near, 0, unroll=4)
            for r in relays:
                r.wait_recv()
            cps += relays
            lax.fori_loop(0, NZ, far, 0, unroll=4)

        ar_b[it, y, c] = tp[c]
        for d, e in ((2, 0), (2, 1), (1, 0), (3, 0), (1, 1), (3, 1), (0, 1)):
            cps.append(
                copy(tp.at[lax.rem(c + e, 2)], ar_b.at[it, y, c], bs.at[it, d, e], br.at[it, d, e], dev(dy=d, dc=e))
            )
            cps[-1].start()
        first_sends = list(cps)
        for d, e in ((0, 1), (1, 0), (3, 0), (1, 1), (3, 1), (2, 0), (2, 1)):
            b = ar_b.at[it, lax.rem(y + NY - d, NY), lax.rem(c + e, 2)]
            copy(b, b, bs.at[it, d, e], br.at[it, d, e], dev(dy=d, dc=e)).wait_recv()
        t = ar_b[it, 0, 0] + ar_b[it, 0, 1]
        for k in range(1, NY):
            t = t + (ar_b[it, k, 0] + ar_b[it, k, 1])
        ar_c[it, z] = t
        for d in (4, 3, 5, 2, 6, 1, 7):
            cps.append(copy(ar_c.at[it, z], ar_c.at[it, z], zs.at[it, d], zr.at[it, d], dev(dz=d)))
            cps[-1].start()
        for d in (1, 7, 2, 6, 3, 5, 4):
            zz = lax.rem(z + NZ - d, NZ)
            copy(ar_c.at[it, zz], ar_c.at[it, zz], zs.at[it, d], zr.at[it, d], dev(dz=d)).wait_recv()
        t = ar_c[it, 0]
        for k in range(1, NZ):
            t = t + ar_c[it, k]
        tot[it, c] = t
        back = copy(tot.at[it, c], tot.at[it, c], ds_.at[it], dr.at[it], dev(dc=1))
        back.start()
        copy(tot.at[it, 1 - c], tot.at[it, 1 - c], ds_.at[it], dr.at[it], dev(dc=1)).wait_recv()
        inv[...] = 1.0 / tot[it]
        cps.append(back)

        def block_of(d):
            return pl.ds(SLOT[(NX - d) % NX] * KC, KC)

        for q, (lo, n) in enumerate(SPLIT):
            cols = pl.ds(lo, n)
            for d in (2, 1, 3, 0):
                if q == 0:
                    macc[...] = jnp.zeros_like(macc)

                    def normalise(zz, carry):
                        w = macc[...]
                        for k in range(2):
                            p = (expo[zz, block_of(d), k * CHUNK : (k + 1) * CHUNK] * inv[k, pl.ds(zz, 1)]).astype(BF)
                            probs[block_of(d), pl.ds(pl.multiple_of(zz * SC + k * CHUNK, CHUNK), CHUNK)] = p
                            p = p.astype(F32)
                            w = w + (p[:, :128] + p[:, 128:])
                        macc[...] = w
                        return carry

                    lax.fori_loop(0, NZ, normalise, 0, unroll=4)
                num = lax.dot_general(
                    probs[block_of(d)], rows[:, :, :, :, cols].reshape(ROWS, n), (((1,), (0,)), ((), ())),
                    preferred_element_type=F32,
                )
                if d:
                    sb[it, d - 1, :, cols] = encode(num)
                    b = (it, d - 1, slice(None), cols)
                    cps.append(copy(sb.at[b], rb.at[b], rs_s.at[it, q, d], rs_r.at[it, q, d], dev(dx=d)))
                    cps[-1].start()
                else:
                    num_own[:, cols] = num
                if q == 0:
                    mass = jnp.sum(macc[...], axis=1, keepdims=True)
                    if d:
                        ms[it, d - 1] = jnp.broadcast_to(mass, (KC, 128)).T[:8]
                        cps.append(copy(ms.at[it, d - 1], mr.at[it, d - 1], ms_s.at[it, d], ms_r.at[it, d], dev(dx=d)))
                        cps[-1].start()

        final = it == ITERS - 1
        if final:

            def slot(other, d, q, half=None):
                part = slice(None) if half is None else pl.ds(half * KC // 2, KC // 2)
                return (1 - yh if other else yh, lax.rem(x + d + NX, NX), part, pl.ds(*SPLIT[q]))

            def go(other, d, k, q, half=None, **to):
                b = coded.at[slot(other, d, q, half)]
                cps.append(copy(b, b, fs.at[q, k], fr.at[q, k], dev(**to)))
                cps[-1].start()

            def come(other, d, k, q, half=None):
                b = coded.at[slot(other, d, q, half)]
                copy(b, b, fs.at[q, k], fr.at[q, k], dev(dc=1)).wait_recv()

            stores = []

            def store(other, d, q):
                b = slot(other, d, q)
                wide[b] = decode(coded[b])
                stores.append(pltpu.make_async_copy(wide.at[b], out.at[b], os_.at[len(stores)]))
                stores[-1].start()

        for q, (lo, n) in enumerate(SPLIT):
            cols = pl.ds(lo, n)
            if q == 0:
                rowm = jnp.zeros((8, 128), F32)
                for d in (1, 3, 2):
                    copy(ms.at[it, d - 1], mr.at[it, d - 1], ms_s.at[it, d], ms_r.at[it, d], dev(dx=d)).wait_recv()
                    rowm = rowm + mr[it, d - 1]
                share = 1.0 / (mass + jnp.broadcast_to(rowm[:1], (KC, 128)).T[:, :1] + PRIOR)
            num = num_own[:, cols] + PRIOR * c_own[:, cols]
            for d in (1, 3, 2):
                b = (it, d - 1, slice(None), cols)
                copy(sb.at[b], rb.at[b], rs_s.at[it, q, d], rs_r.at[it, q, d], dev(dx=d)).wait_recv()
                num = num + decode(rb[b])
            new = num * share
            if not final:
                c_own[:, cols] = new
                cb[it + 1, 0, :, cols] = new.astype(BF)
                for d in (1, 3):
                    b = cb.at[it + 1, 0, :, cols]
                    cps.append(copy(b, cb.at[it + 1, SLOT[d], :, cols], ag_s.at[q, d], ag_r.at[q, d], dev(dx=d)))
                    cps[-1].start()
            else:
                coded[slot(False, 0, q)] = encode(new)
                go(False, 0, 0, q, dy=2)
                go(False, 0, 1, q, dx=1)
                go(False, 0, 2, q, dx=-1)

        if final:
            logs = jnp.log(tot[it, yh])
            for k in range(2):
                tot_out[pl.ds(k, NZ, 2)] = logs[:, k * 128 : (k + 1) * 128]
            for q in range(len(SPLIT)):
                store(False, 0, q)
            for q in range(len(SPLIT)):
                come(False, 1, 2, q)
                go(False, 1, 4, q, dy=2)
                go(False, 1, 7, q, 1, dx=-1)
                come(False, -1, 1, q)
                go(False, -1, 3, q, 0, dx=1)
                come(True, 0, 0, q)
                go(True, 0, 5, q, dx=1)
                store(False, 1, q)
                store(False, -1, q)
            for q in range(len(SPLIT)):
                come(True, 1, 4, q)
                go(True, 1, 6, q, dx=-1)
                store(True, 0, q)
                store(True, 1, q)
            for q in range(len(SPLIT)):
                come(False, 2, 3, q, 0)
                come(False, 2, 7, q, 1)
                store(False, 2, q)
                come(True, -1, 5, q)
                store(True, -1, q)
            for q in range(len(SPLIT)):
                come(True, 2, 6, q)
                store(True, 2, q)
            for st in stores:
                st.wait()
        for cp in cps:
            cp.wait_send()


def hand_on(refined, logs, refined_out, logs_out, held, held_logs, sems):
    parts = [(logs, held_logs, logs_out)]
    parts += [(refined.at[k], held.at[k], refined_out.at[k]) for k in range(2 * NX)]
    into = [pltpu.make_async_copy(a, b, sems.at[0, k]) for k, (a, b, _) in enumerate(parts)]
    back = [pltpu.make_async_copy(b, o, sems.at[1, k]) for k, (_, b, o) in enumerate(parts)]
    for cp in into:
        cp.start()
    for i, o in zip(into, back):
        i.wait()
        o.start()
    for cp in back:
        cp.wait()


def on_device(minibatch, centroids):
    dma = pltpu.SemaphoreType.DMA
    refined, logs = pl.pallas_call(
        body,
        out_shape=(
            jax.ShapeDtypeStruct((2, NX, KC, D), F32),
            jax.ShapeDtypeStruct((2 * NZ, 128), F32),
        ),
        in_specs=[pl.BlockSpec(memory_space=pltpu.VMEM), pl.BlockSpec(memory_space=pl.ANY)],
        out_specs=(pl.BlockSpec(memory_space=pl.ANY), pl.BlockSpec(memory_space=pltpu.VMEM)),
        scratch_shapes=[
            pltpu.VMEM((NZ, NY, NC, BLOCK, D), BF),
            pltpu.VMEM((KD, D), F32),
            pltpu.VMEM((ITERS, NX, KC, D), BF),
            pltpu.VMEM((KC, D), F32),
            pltpu.VMEM((NZ, KD, SC), F32),
            pltpu.VMEM((KD, ROWS), BF),
            pltpu.VMEM((KC, 128), F32),
            pltpu.VMEM((2, NZ, CHUNK), F32),
            pltpu.VMEM((ITERS, NY, NC, NZ, CHUNK), F32),
            pltpu.VMEM((ITERS, NZ, NZ, CHUNK), F32),
            pltpu.VMEM((ITERS, 2, NZ, CHUNK), F32),
            pltpu.VMEM((2, NZ, CHUNK), F32),
            pltpu.VMEM((KC, D), F32),
            pltpu.VMEM((ITERS, 3, KC, D), BF),
            pltpu.VMEM((ITERS, 3, 8, 128), F32),
            pltpu.VMEM((ITERS, 3, KC, D), BF),
            pltpu.VMEM((ITERS, 3, 8, 128), F32),
            pltpu.VMEM((2, NX, KC, D), BF),
            pltpu.VMEM((2, NX, KC, D), F32),
            dma((40,)), dma((NY, NZ, 2)),
            dma((NY, NZ)), dma((NY, NZ)),
            dma((ITERS, NY, NC)), dma((ITERS, NY, NC)),
            dma((ITERS, NZ)), dma((ITERS, NZ)),
            dma((ITERS,)), dma((ITERS,)),
            dma((ITERS, len(SPLIT), NX)), dma((ITERS, len(SPLIT), NX)),
            dma((ITERS, NX)), dma((ITERS, NX)),
            dma((len(SPLIT), NX)), dma((len(SPLIT), NX)),
            dma((len(SPLIT), 8)), dma((len(SPLIT), 8)),
            dma(()), dma((8 * len(SPLIT),)),
        ],
        compiler_params=pltpu.CompilerParams(
            collective_id=0, has_side_effects=True, vmem_limit_bytes=56 * 2**20
        ),
        cost_estimate=pl.CostEstimate(flops=12884901888, bytes_accessed=8 * 2**20, transcendentals=4194304),
        name="em",
    )(minibatch, centroids)
    n = 2 * NX
    refined, logs = pl.pallas_call(
        hand_on,
        out_shape=(jax.ShapeDtypeStruct((n, KC, D), F32), jax.ShapeDtypeStruct((2 * NZ, 128), F32)),
        in_specs=[pl.BlockSpec(memory_space=pl.ANY)] * 2,
        out_specs=[pl.BlockSpec(memory_space=pl.ANY)] * 2,
        scratch_shapes=[
            pltpu.VMEM((n, KC, D), F32),
            pltpu.VMEM((2 * NZ, 128), F32),
            dma((2, n + 1)),
        ],
        name="hand_on",
    )(refined.reshape(n, KC, D), logs)
    return (refined.reshape(n * KC, D), logs.reshape(NZ * CHUNK))


def solution(mesh):
    return jax.shard_map(
        on_device,
        mesh=mesh,
        in_specs=(P(("dp", "cent"), None), P("cent", None)),
        out_specs=(P("cent", None), P("dp")),
        check_vma=False,
    )
```

```python
import functools

import jax
import jax.numpy as jnp
from jax import lax
from jax.experimental import pallas as pl
from jax.experimental.pallas import tpu as pltpu
from jax.sharding import PartitionSpec as P

MESH = pl.DeviceIdType.MESH
ITERS = 2
INV_TEMP = 20.0
PRIOR = 0.5
EPS = 1e-06
LOG2E = 1.4426950408889634
NX, NY, NZ, NC = 4, 4, 8, 2
BLOCK = 64
HALF = BLOCK // 2
CHUNK = 256
SC = 512
ROWS = NZ * SC
SLOT = {0: 0, 1: 1, 3: 2, 2: 3}
SPLIT = ((0, 384), (384, 384))
KC = 128
KD = NX * KC
D = 768
BF = jnp.bfloat16
F32 = jnp.float32


def encode(v):
    s = v * v
    return (v * jnp.abs(v) * s).astype(BF)


def decode(code):
    y = code.astype(F32)
    r = lax.rsqrt(jnp.maximum(jnp.abs(y), 1e-37))
    return y * (r * r * lax.rsqrt(r))


def body(
    mb, cents, out, tot_out,
    rows, cen_in, cb, c_own, expo, probs, macc, tp, ar_b, ar_c, tot, inv,
    num_own, sb, ms, rb, mr, coded, wide,
    gs, gr, cs, cr, bs, br, zs, zr, ds_, dr, rs_s, rs_r, ms_s, ms_r, ag_s, ag_r, fs, fr, loc, os_,
):
    dp, ce = lax.axis_index("dp"), lax.axis_index("cent")
    yh, x = dp // 4, lax.rem(dp, 4)
    z, yl, c = ce // 4, lax.rem(ce, 4) // 2, lax.rem(ce, 2)
    y = yh * 2 + yl

    def dev(dy=0, dx=0, dz=0, dc=0):
        yy, xx = lax.rem(y + dy + NY, NY), lax.rem(x + dx + NX, NX)
        zz, cc = lax.rem(z + dz + NZ, NZ), lax.rem(c + dc, NC)
        return ((yy // 2) * 4 + xx, zz * 4 + lax.rem(yy, 2) * 2 + cc)

    def copy(src, dst, ss, rs, to):
        return pltpu.make_async_remote_copy(
            src_ref=src, dst_ref=dst, send_sem=ss, recv_sem=rs, device_id=to, device_id_type=MESH
        )

    peers = [dict(dc=1)]
    peers += [dict(dy=d) for d in (1, 3)]
    peers += [dict(dx=d) for d in (1, 2, 3)]
    peers += [dict(dz=d) for d in (1, NZ - 1)]
    barrier = pltpu.get_barrier_semaphore()
    for p in peers:
        pl.semaphore_signal(barrier, inc=1, device_id=dev(**p), device_id_type=MESH)
    load = pltpu.make_async_copy(cents.at[pl.ds(yh * KD, KD)], cen_in, loc)
    load.start()

    def unit(v):
        return v * lax.rsqrt(jnp.mean(v * v, axis=-1, keepdims=True) + EPS)

    rows[z, y, c] = unit(mb[...].astype(F32)).astype(BF)
    pl.semaphore_wait(barrier, len(peers))

    scale = INV_TEMP / D * LOG2E
    shift = INV_TEMP * LOG2E

    def score(zz, block, centers, fresh):
        s = lax.dot_general(
            centers, rows[zz].reshape(SC, D), (((1,), (1,)), ((), ())), preferred_element_type=F32
        )
        e = jnp.exp2(s * scale - shift)
        expo[zz, block] = e
        t = jnp.sum(e, axis=0, keepdims=True)
        for k in range(2):
            part = t[:, k * CHUNK : (k + 1) * CHUNK]
            tp[k, pl.ds(zz, 1)] = part if fresh else tp[k, pl.ds(zz, 1)] + part

    def blk(dy, dz, half=None):
        r = rows.at[lax.rem(z + dz + NZ, NZ), lax.rem(y + dy + NY, NY), c]
        return r if half is None else r.at[pl.ds(half * HALF, HALF)]

    def rsem(dy, dz, half=None):
        return gr.at[dy % NY, dz % NZ, half or 0]

    sent = [[], []]

    def lane(first_z, stage):
        sends = sent[0 if first_z else 1]

        def send(dy, dz, ey, ez, half=None):
            b = blk(dy, dz, half)
            copy(b, b, gs.at[len(sends)], rsem(dy - ey, dz - ez, half), dev(dy=ey, dz=ez)).start()
            sends.append((dy, dz, half))

        def landed(dy, dz, half=None):
            b = blk(dy, dz, half)
            copy(b, b, gs.at[0], rsem(dy, dz, half), dev(dc=1)).wait_recv()

        def twin(dy, dz):
            i, j = dy % NY, dz % NZ
            copy(blk(dy, dz), blk(dy, dz), cs.at[i, j], cr.at[i, j], dev(dc=1)).start()

        def along_z(dy, dz):
            if dz == 0:
                send(dy, 0, 0, 1)
                send(dy, 0, 0, -1)
            elif abs(dz) < 3:
                send(dy, dz, 0, 1 if dz < 0 else -1)
            elif abs(dz) == 3:
                send(dy, dz, 0, 1 if dz < 0 else -1, 0 if dz < 0 else 1)

        def along_y(dy, dz):
            if dy == 0:
                send(0, dz, 1, 0)
                send(0, dz, -1, 0)
            elif abs(dy) == 1:
                send(dy, dz, 1 if dy < 0 else -1, 0, 0 if dy < 0 else 1)

        def arrive(dy, dz):
            if abs(dy) == 2 and first_z or dz == 4 and (not first_z or dy == 0) or dy == 2 and dz == 0:
                landed(dy, dz, 0)
                landed(dy, dz, 1)
            else:
                landed(dy, dz)

        if first_z:
            for dz in group(stage):
                if stage:
                    arrive(0, dz)
                along_z(0, dz)
                along_y(0, dz)
                twin(0, dz)
            for dz in group(stage - 1):
                for dy in (-1, 1):
                    arrive(dy, dz)
                    along_y(dy, dz)
                    twin(dy, dz)
            for dz in group(stage - 2):
                arrive(2, dz)
                twin(2, dz)
        elif stage == 0:
            along_y(0, 0)
            along_z(0, 0)
            twin(0, 0)
        else:
            if stage == 1:
                for dy in (-1, 1, 2):
                    arrive(dy, 0)
                    along_y(dy, 0)
                    along_z(dy, 0)
                    twin(dy, 0)
            for dy in (0, -1, 1, 2):
                for dz in group(stage):
                    arrive(dy, dz)
                    along_z(dy, dz)
                    twin(dy, dz)

    def group(s):
        return {0: (0,), 4: (4,)}.get(s, (-s, s)) if 0 <= s <= 4 else ()

    def score_group(s):
        for dz in group(s):
            for i in range(NY):
                his = rows.at[lax.rem(z + dz + NZ, NZ), lax.rem(y + i, NY), 1 - c]
                copy(his, his, cs.at[i, dz % NZ], cr.at[i, dz % NZ], dev(dc=1)).wait_recv()
        for dz in group(s):
            score(lax.rem(z + dz + NZ, NZ), pl.ds(0, KD), cb[0].reshape(KD, D), True)

    for stage in range(7):

        @pl.when(c == 0)
        def _():
            lane(True, stage)

        @pl.when(c == 1)
        def _():
            lane(False, stage)

        if stage == 0:
            load.wait()
            for d in range(NX):
                first = pl.multiple_of(lax.rem(x + NX - d, NX) * KC, KC)
                v = unit(cen_in[pl.ds(first, KC)])
                cb[0, SLOT[d]] = v.astype(BF)
                if d == 0:
                    c_own[...] = v
        score_group(stage - 2)

    def all_sent(sends):
        for k, part in enumerate(sends):
            b = blk(*part)
            copy(b, b, gs.at[k], gr.at[0, 0, 0], dev(dc=1)).wait_send()

    @pl.when(c == 0)
    def _():
        all_sent(sent[0])

    @pl.when(c == 1)
    def _():
        all_sent(sent[1])

    for i in range(NY):
        for j in range(NZ):
            mine = blk(i, j)
            copy(mine, mine, cs.at[i, j], cr.at[i, j], dev(dc=1)).wait_send()

    for it in range(ITERS):
        cps = []
        if it:
            def own(zz, carry):
                score(zz, pl.ds(0, KC), cb[it, 0], True)
                return carry

            def near(zz, carry):
                score(zz, pl.ds(KC, 2 * KC), cb[it, 1:3].reshape(2 * KC, D), False)
                return carry

            def far(zz, carry):
                score(zz, pl.ds(3 * KC, KC), cb[it, 3], False)
                return carry

            lax.fori_loop(0, NZ, own, 0, unroll=4)
            relays = []
            for q, (lo, n) in enumerate(SPLIT):
                cols = pl.ds(lo, n)
                for d, k, half in ((1, 2, 0), (3, 0, 1)):
                    b = cb.at[it, SLOT[d], :, cols]
                    copy(b, b, ag_s.at[q, d], ag_r.at[q, d], dev(dx=d)).wait_recv()
                    part = pl.ds(half * KC // 2, KC // 2)
                    src, dst = cb.at[it, SLOT[d], part, cols], cb.at[it, SLOT[2], part, cols]
                    relays.append(copy(src, dst, ag_s.at[q, k], ag_r.at[q, k], dev(dx=d)))
                    relays[-1].start()
            lax.fori_loop(0, NZ, near, 0, unroll=4)
            for r in relays:
                r.wait_recv()
            cps += relays
            lax.fori_loop(0, NZ, far, 0, unroll=4)

        ar_b[it, y, c] = tp[c]
        for d, e in ((2, 0), (2, 1), (1, 0), (3, 0), (1, 1), (3, 1), (0, 1)):
            cps.append(
                copy(tp.at[lax.rem(c + e, 2)], ar_b.at[it, y, c], bs.at[it, d, e], br.at[it, d, e], dev(dy=d, dc=e))
            )
            cps[-1].start()
        first_sends = list(cps)
        for d, e in ((0, 1), (1, 0), (3, 0), (1, 1), (3, 1), (2, 0), (2, 1)):
            b = ar_b.at[it, lax.rem(y + NY - d, NY), lax.rem(c + e, 2)]
            copy(b, b, bs.at[it, d, e], br.at[it, d, e], dev(dy=d, dc=e)).wait_recv()
        t = ar_b[it, 0, 0] + ar_b[it, 0, 1]
        for k in range(1, NY):
            t = t + (ar_b[it, k, 0] + ar_b[it, k, 1])
        ar_c[it, z] = t
        for d in (4, 3, 5, 2, 6, 1, 7):
            cps.append(copy(ar_c.at[it, z], ar_c.at[it, z], zs.at[it, d], zr.at[it, d], dev(dz=d)))
            cps[-1].start()
        for d in (1, 7, 2, 6, 3, 5, 4):
            zz = lax.rem(z + NZ - d, NZ)
            copy(ar_c.at[it, zz], ar_c.at[it, zz], zs.at[it, d], zr.at[it, d], dev(dz=d)).wait_recv()
        t = ar_c[it, 0]
        for k in range(1, NZ):
            t = t + ar_c[it, k]
        tot[it, c] = t
        back = copy(tot.at[it, c], tot.at[it, c], ds_.at[it], dr.at[it], dev(dc=1))
        back.start()
        copy(tot.at[it, 1 - c], tot.at[it, 1 - c], ds_.at[it], dr.at[it], dev(dc=1)).wait_recv()
        inv[...] = 1.0 / tot[it]
        cps.append(back)

        def block_of(d):
            return pl.ds(SLOT[(NX - d) % NX] * KC, KC)

        for q, (lo, n) in enumerate(SPLIT):
            cols = pl.ds(lo, n)
            for d in (2, 1, 3, 0):
                if q == 0:
                    macc[...] = jnp.zeros_like(macc)

                    def normalise(zz, carry):
                        w = macc[...]
                        for k in range(2):
                            p = (expo[zz, block_of(d), k * CHUNK : (k + 1) * CHUNK] * inv[k, pl.ds(zz, 1)]).astype(BF)
                            probs[block_of(d), pl.ds(pl.multiple_of(zz * SC + k * CHUNK, CHUNK), CHUNK)] = p
                            p = p.astype(F32)
                            w = w + (p[:, :128] + p[:, 128:])
                        macc[...] = w
                        return carry

                    lax.fori_loop(0, NZ, normalise, 0, unroll=4)
                num = lax.dot_general(
                    probs[block_of(d)], rows[:, :, :, :, cols].reshape(ROWS, n), (((1,), (0,)), ((), ())),
                    preferred_element_type=F32,
                )
                if d:
                    sb[it, d - 1, :, cols] = encode(num)
                    b = (it, d - 1, slice(None), cols)
                    cps.append(copy(sb.at[b], rb.at[b], rs_s.at[it, q, d], rs_r.at[it, q, d], dev(dx=d)))
                    cps[-1].start()
                else:
                    num_own[:, cols] = num
                if q == 0:
                    mass = jnp.sum(macc[...], axis=1, keepdims=True)
                    if d:
                        ms[it, d - 1] = jnp.broadcast_to(mass, (KC, 128)).T[:8]
                        cps.append(copy(ms.at[it, d - 1], mr.at[it, d - 1], ms_s.at[it, d], ms_r.at[it, d], dev(dx=d)))
                        cps[-1].start()

        final = it == ITERS - 1
        if final:

            def slot(other, d, q, half=None):
                part = slice(None) if half is None else pl.ds(half * KC // 2, KC // 2)
                return (1 - yh if other else yh, lax.rem(x + d + NX, NX), part, pl.ds(*SPLIT[q]))

            def go(other, d, k, q, half=None, **to):
                b = coded.at[slot(other, d, q, half)]
                cps.append(copy(b, b, fs.at[q, k], fr.at[q, k], dev(**to)))
                cps[-1].start()

            def come(other, d, k, q, half=None):
                b = coded.at[slot(other, d, q, half)]
                copy(b, b, fs.at[q, k], fr.at[q, k], dev(dc=1)).wait_recv()

            stores = []

            def store(other, d, q):
                b = slot(other, d, q)
                wide[b] = decode(coded[b])
                stores.append(pltpu.make_async_copy(wide.at[b], out.at[b], os_.at[len(stores)]))
                stores[-1].start()

        for q, (lo, n) in enumerate(SPLIT):
            cols = pl.ds(lo, n)
            if q == 0:
                rowm = jnp.zeros((8, 128), F32)
                for d in (1, 3, 2):
                    copy(ms.at[it, d - 1], mr.at[it, d - 1], ms_s.at[it, d], ms_r.at[it, d], dev(dx=d)).wait_recv()
                    rowm = rowm + mr[it, d - 1]
                share = 1.0 / (mass + jnp.broadcast_to(rowm[:1], (KC, 128)).T[:, :1] + PRIOR)
            num = num_own[:, cols] + PRIOR * c_own[:, cols]
            for d in (1, 3, 2):
                b = (it, d - 1, slice(None), cols)
                copy(sb.at[b], rb.at[b], rs_s.at[it, q, d], rs_r.at[it, q, d], dev(dx=d)).wait_recv()
                num = num + decode(rb[b])
            new = num * share
            if not final:
                c_own[:, cols] = new
                cb[it + 1, 0, :, cols] = new.astype(BF)
                for d in (1, 3):
                    b = cb.at[it + 1, 0, :, cols]
                    cps.append(copy(b, cb.at[it + 1, SLOT[d], :, cols], ag_s.at[q, d], ag_r.at[q, d], dev(dx=d)))
                    cps[-1].start()
            else:
                coded[slot(False, 0, q)] = encode(new)
                go(False, 0, 0, q, dy=2)
                go(False, 0, 1, q, dx=1)
                go(False, 0, 2, q, dx=-1)

        if final:
            logs = jnp.log(tot[it, yh])
            for k in range(2):
                tot_out[pl.ds(k, NZ, 2)] = logs[:, k * 128 : (k + 1) * 128]
            for q in range(len(SPLIT)):
                store(False, 0, q)
            for q in range(len(SPLIT)):
                come(False, 1, 2, q)
                go(False, 1, 4, q, dy=2)
                go(False, 1, 7, q, 1, dx=-1)
                come(False, -1, 1, q)
                go(False, -1, 3, q, 0, dx=1)
                come(True, 0, 0, q)
                go(True, 0, 5, q, dx=1)
                store(False, 1, q)
                store(False, -1, q)
            for q in range(len(SPLIT)):
                come(True, 1, 4, q)
                go(True, 1, 6, q, dx=-1)
                store(True, 0, q)
                store(True, 1, q)
            for q in range(len(SPLIT)):
                come(False, 2, 3, q, 0)
                come(False, 2, 7, q, 1)
                store(False, 2, q)
                come(True, -1, 5, q)
                store(True, -1, q)
            for q in range(len(SPLIT)):
                come(True, 2, 6, q)
                store(True, 2, q)
            for st in stores:
                st.wait()
        for cp in cps:
            cp.wait_send()


def hand_on(refined, logs, refined_out, logs_out, sems):
    parts = [(logs, logs_out)] + [(refined.at[k], refined_out.at[k]) for k in range(2 * NX)]
    copies = [pltpu.make_async_copy(a, b, sems.at[k]) for k, (a, b) in enumerate(parts)]
    for cp in copies:
        cp.start()
    for cp in copies:
        cp.wait()


def on_device(minibatch, centroids):
    dma = pltpu.SemaphoreType.DMA
    refined, logs = pl.pallas_call(
        body,
        out_shape=(
            jax.ShapeDtypeStruct((2, NX, KC, D), F32),
            jax.ShapeDtypeStruct((2 * NZ, 128), F32),
        ),
        in_specs=[pl.BlockSpec(memory_space=pltpu.VMEM), pl.BlockSpec(memory_space=pl.ANY)],
        out_specs=(pl.BlockSpec(memory_space=pl.ANY), pl.BlockSpec(memory_space=pltpu.VMEM)),
        scratch_shapes=[
            pltpu.VMEM((NZ, NY, NC, BLOCK, D), BF),
            pltpu.VMEM((KD, D), F32),
            pltpu.VMEM((ITERS, NX, KC, D), BF),
            pltpu.VMEM((KC, D), F32),
            pltpu.VMEM((NZ, KD, SC), F32),
            pltpu.VMEM((KD, ROWS), BF),
            pltpu.VMEM((KC, 128), F32),
            pltpu.VMEM((2, NZ, CHUNK), F32),
            pltpu.VMEM((ITERS, NY, NC, NZ, CHUNK), F32),
            pltpu.VMEM((ITERS, NZ, NZ, CHUNK), F32),
            pltpu.VMEM((ITERS, 2, NZ, CHUNK), F32),
            pltpu.VMEM((2, NZ, CHUNK), F32),
            pltpu.VMEM((KC, D), F32),
            pltpu.VMEM((ITERS, 3, KC, D), BF),
            pltpu.VMEM((ITERS, 3, 8, 128), F32),
            pltpu.VMEM((ITERS, 3, KC, D), BF),
            pltpu.VMEM((ITERS, 3, 8, 128), F32),
            pltpu.VMEM((2, NX, KC, D), BF),
            pltpu.VMEM((2, NX, KC, D), F32),
            dma((40,)), dma((NY, NZ, 2)),
            dma((NY, NZ)), dma((NY, NZ)),
            dma((ITERS, NY, NC)), dma((ITERS, NY, NC)),
            dma((ITERS, NZ)), dma((ITERS, NZ)),
            dma((ITERS,)), dma((ITERS,)),
            dma((ITERS, len(SPLIT), NX)), dma((ITERS, len(SPLIT), NX)),
            dma((ITERS, NX)), dma((ITERS, NX)),
            dma((len(SPLIT), NX)), dma((len(SPLIT), NX)),
            dma((len(SPLIT), 8)), dma((len(SPLIT), 8)),
            dma(()), dma((8 * len(SPLIT),)),
        ],
        compiler_params=pltpu.CompilerParams(
            collective_id=0, has_side_effects=True, vmem_limit_bytes=40 * 2**20
        ),
        cost_estimate=pl.CostEstimate(flops=12884901888, bytes_accessed=8 * 2**20, transcendentals=4194304),
        name="em",
    )(minibatch, centroids)
    n = 2 * NX
    refined, logs = pl.pallas_call(
        hand_on,
        out_shape=(jax.ShapeDtypeStruct((n, KC, D), F32), jax.ShapeDtypeStruct((2 * NZ, 128), F32)),
        in_specs=[pl.BlockSpec(memory_space=pl.ANY)] * 2,
        out_specs=[pl.BlockSpec(memory_space=pl.ANY)] * 2,
        scratch_shapes=[dma((n + 1,))],
        compiler_params=pltpu.CompilerParams(vmem_limit_bytes=8 * 2**20),
        name="hand_on",
    )(refined.reshape(n, KC, D), logs)
    return (refined.reshape(n * KC, D), logs.reshape(NZ * CHUNK))


def solution(mesh):
    return jax.shard_map(
        on_device,
        mesh=mesh,
        in_specs=(P(("dp", "cent"), None), P("cent", None)),
        out_specs=(P("cent", None), P("dp")),
        check_vma=False,
    )
```
